256 devices in a mesh: pool: 2 (over y_lo), inst: 4 (over x), tp: 32 (over z, y_hi, core).
Axes of the slice: x: 4, y: 4 (y_hi: 2, y_lo: 2; y = y_hi * 2 + y_lo), z: 8, core: 2. Of those that a mesh axis runs over, the one named last changes fastest.
Arguments:
- hidden_states: bfloat16 [4, 32, 8192], P('inst', None, ('pool', 'tp')), may hold values from -6 to 6
- norm_gain: bfloat16 [8192], P(('pool', 'tp')), may hold values from 0.25 to 1.75
- query_weight: bfloat16 [8192, 4096], P(None, 'tp'), may hold values from -0.0625 to 0.0625
- key_weight: bfloat16 [8192, 512], P(('pool', 'tp')), may hold values from -0.0625 to 0.0625
- value_weight: bfloat16 [8192, 512], P(('pool', 'tp')), may hold values from -0.0625 to 0.0625
- output_weight: bfloat16 [4096, 8192], P('tp'), may hold values from -0.09375 to 0.09375
- key_cache: bfloat16 [2, 4, 32, 128, 512], P('pool', 'inst')
- value_cache: bfloat16 [2, 4, 32, 128, 512], P('pool', 'inst'), may hold values from -24 to 24
- lengths: int32 [4, 32], replicated, may hold values from 1 to 128, as said below
- offload: int32 [4, 32], replicated, may hold values 0 or 1
- host_instance: int32 [4, 32], replicated, may hold values from 0 to 3, as said below
- cache_slot: int32 [4, 32], replicated, may hold values from 0 to 31, as said below
Outputs:
- attention_out: bfloat16 [4, 32, 8192], P('inst', None, ('pool', 'tp'))
The draws below stay inside these ranges and needn't reach their ends.
Inputs may be any that keep to these rules, and one draw needn't show every extreme that they name: `lengths`: each request's context; in every draw some request has exactly 128. `host_instance`: together with cache_slot, no two requests name the same pair. `cache_slot`: together with host_instance, no two requests name the same pair.
All inputs are finite; a program needn't handle non-finite values.
Results may differ from the reference program's by a relative error of at most 0.012.
The reference program's roundings to bfloat16 on the way count: a program that leaves them out, or rounds other values in their place, can miss the bound.
Values may be sent and summed in bfloat16 or wider, within the bound.
No kernel may reach another device: no remote copies, remote signals or barrier semaphores. Data moves between devices by JAX's collectives and lax.ppermute only.
A program may use at most 64 MiB of HBM per device.

```python
import jax
import jax.numpy as jnp
from jax import lax

D = 8192
HD = 128
HQ = 32
CH = 4
REQ = 32
CTX = 128
G = 8
N_POOL = 2
N_INST = 4


def placement_table(key):
    return jax.random.permutation(key, N_INST * REQ).reshape(N_INST, REQ).astype(jnp.int32)


def draw_host_instance(key, part):
    table = placement_table(key)
    return table // REQ


def draw_cache_slot(key, part):
    table = placement_table(key)
    return table % REQ


def draw_lengths(key, part):
    key = jax.random.fold_in(key, 5)
    first_key, second_key = jax.random.split(key)
    drawn = jax.random.randint(first_key, (N_INST * REQ,), 1, CTX + 1).astype(jnp.int32)
    chosen = jax.random.randint(second_key, (), 0, N_INST * REQ).astype(jnp.int32)
    drawn = jnp.where(jnp.arange(N_INST * REQ, dtype=jnp.int32) == chosen, CTX, drawn)
    return drawn.reshape(N_INST, REQ)


def draw_key_cache(key, part):
    key = jax.random.fold_in(key, 11)
    first_key = jax.random.fold_in(key, 0)
    base = jax.random.normal(first_key, (N_POOL, N_INST, REQ, CTX, CH * HD), jnp.float32)
    return base.astype(jnp.bfloat16)


def with_ends(entries, own_key, low, high):
    longest = entries.shape.index(max(entries.shape))
    spots = []
    for shift in (0, 1):
        where = [jax.random.randint(jax.random.fold_in(own_key, axis), (), 0, length) for axis, length in enumerate(entries.shape)]
        where[longest] = (where[longest] + shift) % entries.shape[longest]
        spots.append(tuple(where))
    return entries.at[spots[0]].set(low).at[spots[1]].set(high)


def level_of(own_key, dims, shards, least, largest):
    level, own = 1.0, jax.random.fold_in(own_key, 6)
    for axis_at, parts in shards:
        heights = jnp.exp(jax.random.uniform(jax.random.fold_in(own, axis_at), (parts,), jnp.float32, least / len(shards), largest / len(shards)))
        level = level * jnp.repeat(heights, dims[axis_at] // parts).reshape([-1 if axis == axis_at else 1 for axis in range(len(dims))])
    return level


def bell_draw(rng, shape, scale, reach, cuts=(), kind=jnp.bfloat16):
    loudness = level_of(rng, shape, cuts, -0.22, 0.18) if cuts else 1.0
    array = jax.random.normal(rng, shape, jnp.float32) * scale * loudness
    return jnp.minimum(jnp.maximum(array, -reach), reach).astype(kind)


def setup_inputs(seed: int = 0) -> dict:
    streams_of = jax.random.split(jax.random.key(seed), 13)
    hidden_states = bell_draw(streams_of[0], (N_INST, REQ, D), 1.0, 6.0, ((0, 4), (2, 64)))
    norm_gain = jnp.clip(1.0 + 0.15 * jax.random.normal(streams_of[1], (D,), jnp.float32), 0.25, 1.75).astype(jnp.bfloat16)
    query_weight = bell_draw(streams_of[2], (D, HQ * HD), D ** -0.5, 0.0625, ((1, 32),))
    key_weight = bell_draw(streams_of[3], (D, CH * HD), D ** -0.5, 0.0625, ((0, 64),))
    value_weight = bell_draw(streams_of[4], (D, CH * HD), D ** -0.5, 0.0625, ((0, 64),))
    output_weight = bell_draw(streams_of[5], (HQ * HD, D), (HQ * HD) ** -0.5, 0.09375, ((0, 32),))
    key_cache = draw_key_cache(jax.random.fold_in(streams_of[12], 71), 0)
    value_cache = bell_draw(streams_of[7], (N_POOL, N_INST, REQ, CTX, CH * HD), 4.0, 24.0, ((0, 2), (1, 4)))
    lengths = draw_lengths(jax.random.fold_in(streams_of[12], 71), 0)
    offload = with_ends((jax.random.randint(streams_of[9], (N_INST, REQ), 0, 2) < 1).astype(jnp.int32), jax.random.fold_in(streams_of[9], 1), 0, 1)
    host_instance = draw_host_instance(jax.random.fold_in(streams_of[12], 71), 0)
    cache_slot = draw_cache_slot(jax.random.fold_in(streams_of[12], 71), 0)
    return dict(hidden_states=hidden_states, norm_gain=norm_gain, query_weight=query_weight, key_weight=key_weight, value_weight=value_weight, output_weight=output_weight, key_cache=key_cache, value_cache=value_cache, lengths=lengths, offload=offload, host_instance=host_instance, cache_slot=cache_slot)


epsilon = 1e-05
rope_base = 500000.0

def rotate(values, positions):
    half_width = values.shape[-1] // 2
    frequency = jnp.power(rope_base, -jnp.arange(half_width, dtype=jnp.float32) * 2.0 / values.shape[-1])
    angles = positions.astype(jnp.float32)[:, None] * frequency[None, :]
    cosine_part = jnp.cos(angles)[:, None, :]
    sine_part = jnp.sin(angles)[:, None, :]
    first_half = values[..., :half_width]
    second_half = values[..., half_width:]
    return jnp.concatenate([first_half * cosine_part - second_half * sine_part, first_half * sine_part + second_half * cosine_part], axis=-1)

def reference(hidden_states, norm_gain, query_weight, key_weight, value_weight, output_weight, key_cache, value_cache, lengths, offload, host_instance, cache_slot):
    widened = hidden_states.astype(jnp.float32).reshape(N_INST * REQ, D)
    root = jnp.sqrt(lax.optimization_barrier(jnp.sum(widened * widened, axis=1)) / D + epsilon)
    scaled = (widened * norm_gain.astype(jnp.float32)[None, :]).astype(jnp.bfloat16)
    positions = lengths.reshape(-1)
    queries = jnp.dot(scaled, query_weight, preferred_element_type=jnp.float32) / root[:, None]
    keys_raw = jnp.dot(scaled, key_weight, preferred_element_type=jnp.float32) / root[:, None]
    values_raw = jnp.dot(scaled, value_weight, preferred_element_type=jnp.float32) / root[:, None]
    queries = rotate(queries.reshape(-1, HQ, HD), positions).astype(jnp.bfloat16)
    new_keys = rotate(keys_raw.reshape(-1, CH, HD), positions).astype(jnp.bfloat16)
    new_values = values_raw.reshape(-1, CH, HD).astype(jnp.bfloat16)
    request_ids = jnp.arange(N_INST * REQ, dtype=jnp.int32)
    flags = offload.reshape(-1).astype(jnp.int32)
    instances = jnp.where(flags == 1, host_instance.reshape(-1), request_ids // REQ).astype(jnp.int32)
    slots_used = jnp.where(flags == 1, cache_slot.reshape(-1), request_ids % REQ).astype(jnp.int32)
    factor = HD ** (-0.5)

    def attend_one(index):
        chosen_keys = key_cache[flags[index], instances[index], slots_used[index]].astype(jnp.float32).reshape(CTX, CH, HD)
        chosen_values = value_cache[flags[index], instances[index], slots_used[index]].astype(jnp.float32).reshape(CTX, CH, HD)
        query_rows = queries[index].astype(jnp.float32).reshape(CH, G, HD)
        scores = jnp.einsum('cgd,pcd->cgp', query_rows, chosen_keys) * factor
        own_score = jnp.einsum('cgd,cd->cg', query_rows, new_keys[index].astype(jnp.float32)) * factor
        visible = (jnp.arange(CTX, dtype=jnp.int32) < positions[index])[None, None, :]
        peak = jnp.maximum(lax.optimization_barrier(jnp.max(jnp.where(visible, scores, -jnp.inf), axis=-1)), own_score)
        exps = jnp.where(visible, jnp.exp(scores - peak[..., None]), 0.0)
        own_exp = jnp.exp(own_score - peak)
        denominator = lax.optimization_barrier(jnp.sum(exps, axis=-1)) + own_exp
        weights_soft = (exps / denominator[..., None]).astype(jnp.bfloat16)
        own_weight = (own_exp / denominator).astype(jnp.bfloat16)
        mixed = jnp.einsum('cgp,pcd->cgd', weights_soft.astype(jnp.float32), chosen_values)
        mixed = mixed + own_weight.astype(jnp.float32)[..., None] * new_values[index].astype(jnp.float32)[:, None, :]
        return mixed.astype(jnp.bfloat16).reshape(HQ * HD)
    attended = lax.map(attend_one, request_ids)
    result = jnp.dot(attended, output_weight, preferred_element_type=jnp.float32)
    return result.astype(jnp.bfloat16).reshape(N_INST, REQ, D)
```

```python
import jax
import jax.numpy as jnp
import numpy as np
from jax import lax
from jax.sharding import Mesh
from jax.sharding import PartitionSpec as P

HD = 128
G = 8
epsilon = 1e-05
rope_base = 500000.0
AXES = ("pool", "inst", "z", "yh", "core")
SIZES = (2, 4, 8, 2, 2)
TP = ("z", "yh", "core")
RING = ("z", "yh")
BF = jnp.bfloat16
F32 = jnp.float32


def swap_core(x):
    return lax.ppermute(x, "core", [(0, 1), (1, 0)])


def shards(
    hidden_states,
    norm_gain,
    query_weight,
    key_weight,
    value_weight,
    output_weight,
    key_cache,
    value_cache,
    lengths,
    offload,
    host_instance,
    cache_slot,
):
    pool = lax.axis_index("pool")
    inst = lax.axis_index("inst")
    z = lax.axis_index("z")
    core = lax.axis_index("core")
    rows = hidden_states.shape[1]
    width = query_weight.shape[0]
    half = width // 2
    ring = SIZES[2] * SIZES[3]

    x = hidden_states[0].astype(F32)
    scaled = (x * norm_gain.astype(F32)[None, :]).astype(BF)
    squares = jnp.sum(x * x, axis=1)
    high = squares.astype(BF)
    low = (squares - high.astype(F32)).astype(BF)
    extra = jnp.zeros((16, HD), BF).at[0, :rows].set(high).at[1, :rows].set(low)
    k_terms = jnp.dot(scaled, key_weight, preferred_element_type=F32).astype(BF)
    v_terms = jnp.dot(scaled, value_weight, preferred_element_type=F32).astype(BF)

    def by_peer(t):
        t = t.reshape(rows, 4, HD).transpose(1, 0, 2)
        return jnp.repeat(t, ring // 4, axis=0)

    message = jnp.concatenate(
        [
            jnp.broadcast_to(scaled[None], (ring, rows, HD)),
            by_peer(k_terms),
            by_peer(v_terms),
            jnp.broadcast_to(extra[None], (ring, 16, HD)),
        ],
        axis=1,
    )
    got = lax.all_to_all(message, RING, 0, 0, tiled=True)
    other = swap_core(got)
    core0 = jnp.where(core == 0, got, other)
    core1 = jnp.where(core == 0, other, got)
    both = jnp.stack([core0, core1], axis=1).reshape(2 * ring, -1, HD)

    tokens = both[:, :rows].transpose(1, 0, 2).reshape(rows, half)
    weight = lax.dynamic_slice_in_dim(query_weight, pool * half, half, 0)
    q_part = jnp.dot(tokens, weight, preferred_element_type=F32)
    sums = jnp.sum(both[:, rows:].astype(F32), axis=0)
    squares = sums[2 * rows, :rows] + sums[2 * rows + 1, :rows]
    high = squares.astype(BF)
    low = (squares - high.astype(F32)).astype(BF)
    lane = jnp.arange(HD)[None, :]
    extra = jnp.where(lane < HD // 2, high[:, None], low[:, None])
    message = jnp.concatenate([q_part.astype(BF), sums[: 2 * rows].astype(BF), extra], axis=0)
    message = jnp.broadcast_to(message[None], (8, 4 * rows, HD))
    got = lax.all_to_all(message, ("pool", "inst"), 0, 0, tiled=True)

    flags = offload.reshape(-1)
    hosts = host_instance.reshape(-1)
    slots = cache_slot.reshape(-1)
    spans = lengths.reshape(-1)
    request = jnp.arange(flags.shape[0], dtype=jnp.int32)
    slot = jnp.arange(rows, dtype=jnp.int32)[:, None]
    hosted = (flags == 1)[None, :] & (hosts == inst)[None, :] & (slots[None, :] == slot)
    resident = request[None, :] == inst * rows + slot
    chosen = jnp.where(pool == 1, hosted, resident)
    positions = jnp.sum(jnp.where(chosen, spans[None, :], 0), axis=1)
    pick = chosen.astype(BF)
    pick = jnp.concatenate([pick, pick], axis=1)
    parts = got.reshape(8, 4, rows, HD).transpose(0, 2, 1, 3).reshape(8 * rows, 4 * HD)
    mine = jnp.dot(pick, parts, preferred_element_type=F32)
    q, k, v, s = jnp.split(mine, 4, axis=1)
    squares = s[:, 0] + s[:, HD // 2]
    root = jnp.sqrt(squares / width + epsilon)[:, None]
    frequency = jnp.asarray(
        np.power(np.float32(rope_base), -np.arange(HD // 2, dtype=np.float32) * 2.0 / HD).astype(np.float32)
    )
    angles = positions.astype(F32)[:, None] * frequency[None, :]
    cosine, sine = jnp.cos(angles), jnp.sin(angles)

    def rotate(t):
        a, b = t[:, : HD // 2], t[:, HD // 2 :]
        return jnp.concatenate([a * cosine - b * sine, a * sine + b * cosine], axis=1)

    q = rotate(q / root).astype(BF)
    k = rotate(k / root).astype(BF)
    v = (v / root).astype(BF)

    start = (z // 2) * HD
    keys = lax.dynamic_slice_in_dim(key_cache[0, 0], start, HD, 2)
    values = lax.dynamic_slice_in_dim(value_cache[0, 0], start, HD, 2)
    factor = HD ** (-0.5)
    scores = jnp.einsum("rd,rpd->rp", q, keys, preferred_element_type=F32) * factor
    own_score = jnp.sum(q.astype(F32) * k.astype(F32), axis=1, keepdims=True) * factor
    visible = jnp.arange(keys.shape[1])[None, :] < positions[:, None]
    peak = jnp.maximum(jnp.max(jnp.where(visible, scores, -jnp.inf), axis=1, keepdims=True), own_score)
    exps = jnp.where(visible, jnp.exp(scores - peak), 0.0)
    own_exp = jnp.exp(own_score - peak)
    total = jnp.sum(exps, axis=1, keepdims=True) + own_exp
    weights = (exps / total).astype(BF)
    own_weight = (own_exp / total).astype(BF)
    mixed = jnp.einsum("rp,rpd->rd", weights, values, preferred_element_type=F32)
    mixed = (mixed + own_weight.astype(F32) * v.astype(F32)).astype(BF)

    got = lax.all_to_all(jnp.broadcast_to(mixed[None], (8, rows, HD)), ("pool", "inst"), 0, 0, tiled=True)
    flags_own = lax.dynamic_index_in_dim(offload, inst, 0, keepdims=False)
    hosts_own = lax.dynamic_index_in_dim(host_instance, inst, 0, keepdims=False)
    slots_own = lax.dynamic_index_in_dim(cache_slot, inst, 0, keepdims=False)
    place = jnp.where(flags_own == 1, (4 + hosts_own) * rows + slots_own, inst * rows + slot[:, 0])
    back = (place[:, None] == jnp.arange(8 * rows, dtype=jnp.int32)[None, :]).astype(BF)
    attended = jnp.dot(back, got.reshape(8 * rows, HD), preferred_element_type=F32).astype(BF)

    weight = lax.dynamic_slice_in_dim(output_weight, pool * half, half, 1)
    partial = jnp.dot(attended, weight, preferred_element_type=F32).astype(BF)
    partial = partial.reshape(rows, ring, 2, HD).transpose(2, 1, 0, 3)
    keep = lax.dynamic_index_in_dim(partial, core, 0, keepdims=False)
    give = lax.dynamic_index_in_dim(partial, 1 - core, 0, keepdims=False)
    pair = (keep.astype(F32) + swap_core(give).astype(F32)).astype(BF)
    got = lax.all_to_all(pair, RING, 0, 0, tiled=True)
    return jnp.sum(got.astype(F32), axis=0).astype(BF)[None]


def solution(mesh):
    finer = Mesh(mesh.devices.reshape(SIZES), AXES)
    in_specs = (
        P("inst", None, ("pool",) + TP),
        P(("pool",) + TP),
        P(None, TP),
        P(("pool",) + TP, None),
        P(("pool",) + TP, None),
        P(TP, None),
        P("pool", "inst", None, None, None),
        P("pool", "inst", None, None, None),
        P(),
        P(),
        P(),
        P(),
    )
    out_specs = P("inst", None, ("pool",) + TP)
    return jax.shard_map(shards, mesh=finer, in_specs=in_specs, out_specs=out_specs, check_vma=False)
```

```python
import functools

import jax
import jax.numpy as jnp
from jax import lax
from jax.experimental import pallas as pl
from jax.experimental.pallas import tpu as pltpu
from jax.sharding import Mesh
from jax.sharding import PartitionSpec as P

HD = 128
HEADS = 4
REQ = 32
POOLS, INSTS, ZS, YS, CORES = 2, 4, 8, 2, 2
RING = ZS * POOLS
epsilon = 1e-05
rope_base = 500000.0
AXES = ("pool", "inst", "z", "yh", "core")
SIZES = (POOLS, INSTS, ZS, YS, CORES)
TP = ("z", "yh", "core")
BF = jnp.bfloat16
F32 = jnp.float32
I32 = jnp.int32
VMEM = pl.BlockSpec(memory_space=pltpu.VMEM)
ANY = pl.BlockSpec(memory_space=pl.ANY)


def device_number(p, i, z, y, c):
    return (((p * INSTS + i) * ZS + z) * YS + y) * CORES + c


RINGS = [
    [device_number(p, i, z, p ^ s, c) for z in range(ZS) for p in range(POOLS)]
    for s in range(2)
    for i in range(INSTS)
    for c in range(CORES)
]


def ring_exchange(x):
    return lax.all_to_all(x, AXES, 0, 0, axis_index_groups=RINGS, tiled=True)


def swap_core(x):
    return lax.ppermute(x, "core", [(0, 1), (1, 0)])


def iota(shape, axis):
    return lax.broadcasted_iota(I32, shape, axis)


def dot(a, b):
    return jnp.dot(a, b, preferred_element_type=F32)


def split(x):
    high = x.astype(BF)
    return high, (x - high.astype(F32)).astype(BF)


def features_kernel(x_ref, gain_ref, wk_ref, wv_ref, out_ref):
    x = x_ref[0].astype(F32)
    scaled = (x * gain_ref[...].astype(F32)).astype(BF)
    squares = jnp.sum(x * x, axis=1, keepdims=True)
    eye = iota((REQ, HD), 0) == iota((REQ, HD), 1)
    row = jnp.sum(jnp.where(eye, squares, 0.0), axis=0, keepdims=True)
    high = row.astype(BF).astype(F32)
    at = iota((16, HD), 0)
    extra = jnp.where(at == 0, high, jnp.where(at == 1, row - high, 0.0)).astype(BF)
    k = dot(scaled, wk_ref[...]).astype(BF)
    v = dot(scaled, wv_ref[...]).astype(BF)
    for m in range(RING):
        head = slice((m // POOLS) // (ZS // HEADS) * HD, ((m // POOLS) // (ZS // HEADS) + 1) * HD)
        out_ref[m, 0:REQ, :] = scaled
        out_ref[m, REQ : 2 * REQ, :] = k[:, head]
        out_ref[m, 2 * REQ : 3 * REQ, :] = v[:, head]
        out_ref[m, 3 * REQ :, :] = extra


def query_kernel(own_ref, other_ref, wq_ref, out_ref):
    pool, yh, core = lax.axis_index("pool"), lax.axis_index("yh"), lax.axis_index("core")
    side = pool ^ yh
    q = jnp.zeros((REQ, HD), F32)
    sums = jnp.zeros((2 * REQ, HD), F32)
    extra = jnp.zeros((16, HD), F32)
    for m in range(RING):
        z, p = m // POOLS, m % POOLS
        y = p ^ side
        features = jnp.concatenate([own_ref[m, 0:REQ, :], other_ref[m, 0:REQ, :]], axis=1)
        weight = jnp.concatenate([wq_ref[p, z, y, core], wq_ref[p, z, y, 1 - core]], axis=0)
        q += dot(features, weight)
        sums += own_ref[m, REQ : 3 * REQ, :].astype(F32) + other_ref[m, REQ : 3 * REQ, :].astype(F32)
        extra += own_ref[m, 3 * REQ :, :].astype(F32) + other_ref[m, 3 * REQ :, :].astype(F32)
    row = extra[0:1] + extra[1:2]
    eye = iota((REQ, HD), 0) == iota((REQ, HD), 1)
    squares = jnp.sum(jnp.where(eye, row, 0.0), axis=1, keepdims=True)
    high = squares.astype(BF).astype(F32)
    tail = jnp.where(iota((REQ, HD), 1) < HD // 2, high, squares - high)
    message = jnp.concatenate([q, sums[:REQ], sums[REQ:], tail], axis=1).astype(BF)
    for m in range(POOLS * INSTS):
        out_ref[m] = message


def tables_kernel(
    lengths_ref, offload_ref, host_ref, slot_ref, keys_ref, values_ref,
    keys_out, values_out, pick_ref, back_ref, cos_ref, sin_ref, span_ref, sems,
):
    pool, inst, z = lax.axis_index("pool"), lax.axis_index("inst"), lax.axis_index("z")
    lane = pl.ds(pl.multiple_of((z // (ZS // HEADS)) * HD, HD), HD)
    copies = [
        pltpu.make_async_copy(keys_ref.at[0, 0, :, :, lane], keys_out, sems.at[0]),
        pltpu.make_async_copy(values_ref.at[0, 0, :, :, lane], values_out, sems.at[1]),
    ]
    for copy in copies:
        copy.start()
    home = iota((INSTS, REQ), 0) * REQ + iota((INSTS, REQ), 1)
    away = INSTS * REQ + host_ref[...] * REQ + slot_ref[...]
    seat = jnp.where(offload_ref[...] == 1, away, home)
    spans = lengths_ref[...].astype(F32)
    here = iota((REQ, REQ), 0) + (pool * INSTS + inst) * REQ
    square = iota((REQ, REQ), 0) == iota((REQ, REQ), 1)
    pick = jnp.zeros((REQ, POOLS * INSTS * REQ), F32)
    span = jnp.zeros((REQ, 1), F32)
    column = jnp.zeros((REQ, 1), F32)
    for i in range(INSTS):
        sits = seat[i : i + 1, :] == here
        wide = iota((REQ, POOLS * INSTS * REQ), 1) % (INSTS * REQ)
        place = (wide == iota(wide.shape, 0) + i * REQ).astype(F32).astype(BF)
        pick += dot(sits.astype(F32).astype(BF), place)
        span += jnp.sum(jnp.where(sits, spans[i : i + 1, :], 0.0), axis=1, keepdims=True)
        turned = jnp.sum(jnp.where(square, seat[i : i + 1, :].astype(F32), 0.0), axis=1, keepdims=True)
        column += jnp.where(inst == i, turned, 0.0)
    pick_ref[...] = pick.astype(BF)
    seats = iota((REQ, POOLS * INSTS * REQ), 1).astype(F32)
    back_ref[...] = (column == seats).astype(F32).astype(BF)
    half = HD // 2
    lanes = iota((REQ, HD), 1)
    frequency = jnp.exp((lanes % half).astype(F32) * (-2.0 / HD * 13.122363377404328))
    angles = span * frequency
    cos_ref[...] = jnp.cos(angles)
    sin_ref[...] = jnp.where(lanes < half, -jnp.sin(angles), jnp.sin(angles))
    span_ref[...] = jnp.broadcast_to(span, (REQ, HD))
    for copy in copies:
        copy.wait()


def attend_kernel(got_ref, keys_ref, values_ref, pick_ref, cos_ref, sin_ref, span_ref, out_ref, *, width):
    got = got_ref[...].reshape(POOLS * INSTS * REQ, 4 * HD)
    mine = dot(pick_ref[...], got)
    q, k, v, s = (mine[:, n * HD : (n + 1) * HD] for n in range(4))
    squares = s[:, 0:1] + s[:, HD // 2 : HD // 2 + 1]
    root = jnp.sqrt(squares / width + epsilon)

    def rotate(t):
        return t * cos_ref[...] + pltpu.roll(t, HD // 2, 1) * sin_ref[...]

    q = rotate(q / root).astype(BF)
    k = rotate(k / root).astype(BF)
    v = (v / root).astype(BF)
    keys = keys_ref[...].reshape(REQ * HD, HD)
    values = values_ref[...].reshape(REQ * HD, HD)
    every = lax.dot_general(q, keys, (((1,), (1,)), ((), ())), preferred_element_type=F32)
    request = iota((8, HD), 0)
    rows = []
    for group in range(REQ // 8):
        block = jnp.zeros((8, HD), F32)
        for n in range(8):
            r = group * 8 + n
            block = jnp.where(request == n, every[group * 8 : group * 8 + 8, r * HD : (r + 1) * HD], block)
        rows.append(block)
    factor = HD ** (-0.5)
    scores = jnp.concatenate(rows, axis=0) * factor
    own_score = jnp.sum(q.astype(F32) * k.astype(F32), axis=1, keepdims=True) * factor
    visible = iota((REQ, HD), 1).astype(F32) < span_ref[...]
    scores = jnp.where(visible, scores, -jnp.inf)
    peak = jnp.maximum(jnp.max(scores, axis=1, keepdims=True), own_score)
    exps = jnp.exp(scores - peak)
    own_exp = jnp.exp(own_score - peak)
    total = jnp.sum(exps, axis=1, keepdims=True) + own_exp
    weights = exps / total
    own_weight = (own_exp / total).astype(BF).astype(F32)
    request = iota((REQ, HD), 0)
    spread = jnp.concatenate([jnp.where(request == r, weights, 0.0).astype(BF) for r in range(REQ)], axis=1)
    mixed = (dot(spread, values) + own_weight * v.astype(F32)).astype(BF)
    for m in range(POOLS * INSTS * CORES):
        out_ref[m] = mixed


def output_kernel(got_ref, back_ref, own_ref, other_ref, out_ref):
    pool, yh, core = lax.axis_index("pool"), lax.axis_index("yh"), lax.axis_index("core")
    side = pool ^ yh
    back = back_ref[...]
    seats = POOLS * INSTS * REQ
    mine = dot(back, got_ref[:, core].reshape(seats, HD)).astype(BF)
    buddy = dot(back, got_ref[:, 1 - core].reshape(seats, HD)).astype(BF)
    rows = jnp.concatenate([mine, buddy], axis=1)
    for m in range(RING):
        z, p = m // POOLS, m % POOLS
        block = ((p * ZS + z) * YS + (p ^ side)) * CORES + core
        lane = pl.ds(pl.multiple_of(block * HD, HD), HD)
        weight = jnp.concatenate([own_ref[:, lane], other_ref[:, lane]], axis=0)
        out_ref[m] = dot(rows, weight).astype(BF)


def sum_kernel(got_ref, out_ref):
    total = got_ref[0].astype(F32)
    for m in range(1, RING):
        total += got_ref[m].astype(F32)
    out_ref[0] = total.astype(BF)


def call(kernel, shapes, specs, flops, moved, scratch=(), limit=24):
    one = not isinstance(shapes, list)
    return pl.pallas_call(
        kernel,
        out_shape=shapes if one else tuple(shapes),
        in_specs=specs,
        out_specs=VMEM if one else tuple(VMEM for _ in shapes),
        scratch_shapes=list(scratch),
        cost_estimate=pl.CostEstimate(flops=flops, bytes_accessed=moved, transcendentals=0),
        compiler_params=pltpu.CompilerParams(vmem_limit_bytes=limit << 20),
    )


def shape(*dims, dtype=BF):
    return jax.ShapeDtypeStruct(dims, dtype)


def shards(
    hidden_states,
    norm_gain,
    query_weight,
    key_weight,
    value_weight,
    output_weight,
    key_cache,
    value_cache,
    lengths,
    offload,
    host_instance,
    cache_slot,
):
    width = query_weight.shape[0]
    seats = POOLS * INSTS * REQ

    message = call(features_kernel, shape(RING, 3 * REQ + 16, HD), [VMEM] * 4, 1 << 23, 1 << 20)(
        hidden_states, norm_gain.reshape(1, HD), key_weight, value_weight
    )
    buddy_weight = swap_core(output_weight)
    got = ring_exchange(message)
    other = swap_core(got)
    message = call(query_kernel, shape(POOLS * INSTS, REQ, 4 * HD), [VMEM] * 3, 1 << 25, 1 << 22)(
        got, other, query_weight.reshape(POOLS, ZS, YS, CORES, HD, HD)
    )
    keys, values, pick, back, cos, sin, span = call(
        tables_kernel,
        [
            shape(REQ, HD, HD),
            shape(REQ, HD, HD),
            shape(REQ, seats),
            shape(REQ, seats),
            shape(REQ, HD, dtype=F32),
            shape(REQ, HD, dtype=F32),
            shape(REQ, HD, dtype=F32),
        ],
        [VMEM] * 4 + [ANY] * 2,
        1 << 22,
        1 << 23,
        [pltpu.SemaphoreType.DMA((2,))],
    )(lengths, offload, host_instance, cache_slot, key_cache, value_cache)
    got = lax.all_to_all(message, ("pool", "inst"), 0, 0, tiled=True)
    message = call(
        functools.partial(attend_kernel, width=width), shape(POOLS * INSTS * CORES, REQ, HD), [VMEM] * 7, 1 << 26, 1 << 22
    )(got, keys, values, pick, cos, sin, span)
    got = lax.all_to_all(message, ("pool", "inst", "core"), 0, 0, tiled=True)
    message = call(output_kernel, shape(RING, REQ, HD), [VMEM] * 4, 1 << 25, 1 << 22)(
        got.reshape(POOLS * INSTS, CORES, REQ, HD), back, output_weight, buddy_weight
    )
    got = ring_exchange(message)
    return call(sum_kernel, shape(1, REQ, HD), [VMEM], 1 << 17, 1 << 18)(got)


def solution(mesh):
    finer = Mesh(mesh.devices.reshape(SIZES), AXES)
    in_specs = (
        P("inst", None, ("pool",) + TP),
        P(("pool",) + TP),
        P(None, TP),
        P(("pool",) + TP, None),
        P(("pool",) + TP, None),
        P(TP, None),
        P("pool", "inst", None, None, None),
        P("pool", "inst", None, None, None),
        P(),
        P(),
        P(),
        P(),
    )
    out_specs = P("inst", None, ("pool",) + TP)
    return jax.shard_map(shards, mesh=finer, in_specs=in_specs, out_specs=out_specs, check_vma=False)
```

```python
import functools

import jax
import jax.numpy as jnp
from jax import lax
from jax.experimental import pallas as pl
from jax.experimental.pallas import tpu as pltpu
from jax.sharding import Mesh
from jax.sharding import PartitionSpec as P

HD = 128
HEADS = 4
REQ = 32
POOLS, INSTS, ZS, YS, CORES = 2, 4, 8, 2, 2
RING = ZS * POOLS
epsilon = 1e-05
rope_base = 500000.0
AXES = ("pool", "inst", "z", "yh", "core")
SIZES = (POOLS, INSTS, ZS, YS, CORES)
TP = ("z", "yh", "core")
BF = jnp.bfloat16
F32 = jnp.float32
I32 = jnp.int32
VMEM = pl.BlockSpec(memory_space=pltpu.VMEM)
HBM = pl.BlockSpec(memory_space=pltpu.HBM)


def device_number(p, i, z, y, c):
    return (((p * INSTS + i) * ZS + z) * YS + y) * CORES + c


RINGS = [
    [device_number(p, i, z, p ^ s, c) for z in range(ZS) for p in range(POOLS)]
    for s in range(2)
    for i in range(INSTS)
    for c in range(CORES)
]


def ring_exchange(x):
    return lax.all_to_all(x, AXES, 0, 0, axis_index_groups=RINGS, tiled=True)


def swap_core(x):
    return lax.ppermute(x, "core", [(0, 1), (1, 0)])


def iota(shape, axis):
    return lax.broadcasted_iota(I32, shape, axis)


def dot(a, b):
    return jnp.dot(a, b, preferred_element_type=F32)


def split(x):
    high = x.astype(BF)
    return high, (x - high.astype(F32)).astype(BF)


def start_copies(pairs, sems):
    copies = [pltpu.make_async_copy(a, b, sems.at[n]) for n, (a, b) in enumerate(pairs)]
    for copy in copies:
        copy.start()
    return copies


def head_lanes(z):
    return pl.ds(pl.multiple_of((z // (ZS // HEADS)) * HD, HD), HD)


def features_kernel(x_hbm, gain_hbm, wk_hbm, wv_hbm, out_ref, x_ref, gain_ref, wk_ref, wv_ref, sems):
    pairs = ((x_hbm, x_ref), (gain_hbm, gain_ref), (wk_hbm, wk_ref), (wv_hbm, wv_ref))
    for copy in start_copies(pairs, sems):
        copy.wait()
    x = x_ref[0].astype(F32)
    scaled = (x * gain_ref[...].astype(F32)).astype(BF)
    squares = jnp.sum(x * x, axis=1, keepdims=True)
    eye = iota((REQ, HD), 0) == iota((REQ, HD), 1)
    row = jnp.sum(jnp.where(eye, squares, 0.0), axis=0, keepdims=True)
    high = row.astype(BF).astype(F32)
    at = iota((16, HD), 0)
    extra = jnp.where(at == 0, high, jnp.where(at == 1, row - high, 0.0)).astype(BF)
    k = dot(scaled, wk_ref[...]).astype(BF)
    v = dot(scaled, wv_ref[...]).astype(BF)
    for m in range(RING):
        n = (m // POOLS) // (ZS // HEADS)
        head = slice(n * HD, (n + 1) * HD)
        out_ref[m, 0:REQ, :] = scaled
        out_ref[m, REQ : 2 * REQ, :] = k[:, head]
        out_ref[m, 2 * REQ : 3 * REQ, :] = v[:, head]
        out_ref[m, 3 * REQ :, :] = extra


def early_kernel(
    lengths_hbm, offload_hbm, host_hbm, slot_hbm, keys_hbm, wq_hbm,
    keys_out, wq_out, pick_ref, back_ref, cos_ref, sin_ref, span_ref,
    lengths_ref, offload_ref, host_ref, slot_ref, sems,
):
    pool, inst, z = lax.axis_index("pool"), lax.axis_index("inst"), lax.axis_index("z")
    core = lax.axis_index("core")
    side = pool ^ lax.axis_index("yh")
    pairs = [(lengths_hbm, lengths_ref), (offload_hbm, offload_ref), (host_hbm, host_ref), (slot_hbm, slot_ref)]
    small = len(pairs)
    for p in range(POOLS):
        for n, c in enumerate((core, 1 - core)):
            pairs.append((wq_hbm.at[p, :, p ^ side, c], wq_out.at[:, p, pl.ds(n * HD, HD), :]))
    pairs.append((keys_hbm.at[0, 0, :, :, head_lanes(z)], keys_out))
    copies = start_copies(pairs, sems)
    for copy in copies[:small]:
        copy.wait()
    home = iota((INSTS, REQ), 0) * REQ + iota((INSTS, REQ), 1)
    away = INSTS * REQ + host_ref[...] * REQ + slot_ref[...]
    seat = jnp.where(offload_ref[...] == 1, away, home)
    spans = lengths_ref[...].astype(F32)
    here = iota((REQ, REQ), 0) + (pool * INSTS + inst) * REQ
    square = iota((REQ, REQ), 0) == iota((REQ, REQ), 1)
    pick = jnp.zeros((REQ, POOLS * INSTS * REQ), F32)
    span = jnp.zeros((REQ, 1), F32)
    column = jnp.zeros((REQ, 1), F32)
    for i in range(INSTS):
        sits = seat[i : i + 1, :] == here
        wide = iota((REQ, POOLS * INSTS * REQ), 1) % (INSTS * REQ)
        place = (wide == iota(wide.shape, 0) + i * REQ).astype(F32).astype(BF)
        pick += dot(sits.astype(F32).astype(BF), place)
        span += jnp.sum(jnp.where(sits, spans[i : i + 1, :], 0.0), axis=1, keepdims=True)
        turned = jnp.sum(jnp.where(square, seat[i : i + 1, :].astype(F32), 0.0), axis=1, keepdims=True)
        column += jnp.where(inst == i, turned, 0.0)
    pick_ref[...] = pick.astype(BF)
    seats = iota((REQ, POOLS * INSTS * REQ), 1).astype(F32)
    back_ref[...] = (column == seats).astype(F32).astype(BF)
    half = HD // 2
    lanes = iota((REQ, HD), 1)
    frequency = jnp.exp((lanes % half).astype(F32) * (-2.0 / HD * 13.122363377404328))
    angles = span * frequency
    cos_ref[...] = jnp.cos(angles)
    sin_ref[...] = jnp.where(lanes < half, -jnp.sin(angles), jnp.sin(angles))
    span_ref[...] = jnp.broadcast_to(span, (REQ, HD))
    for copy in copies[small:]:
        copy.wait()


def late_kernel(values_hbm, own_hbm, other_hbm, values_out, own_out, other_out, sems):
    core = lax.axis_index("core")
    side = lax.axis_index("pool") ^ lax.axis_index("yh")
    pairs = [(values_hbm.at[0, 0, :, :, head_lanes(lax.axis_index("z"))], values_out)]
    for source, out in ((own_hbm, own_out), (other_hbm, other_out)):
        for m in range(RING):
            z, p = m // POOLS, m % POOLS
            block = ((p * ZS + z) * YS + (p ^ side)) * CORES + core
            lanes = pl.ds(pl.multiple_of(block * HD, HD), HD)
            pairs.append((source.at[:, lanes], out.at[:, pl.ds(m * HD, HD)]))
    for copy in start_copies(pairs, sems):
        copy.wait()


def query_kernel(own_ref, other_ref, wq_ref, out_ref):
    q = jnp.zeros((REQ, HD), F32)
    sums = jnp.zeros((2 * REQ, HD), F32)
    extra = jnp.zeros((16, HD), F32)
    for m in range(RING):
        features = jnp.concatenate([own_ref[m, 0:REQ, :], other_ref[m, 0:REQ, :]], axis=1)
        q += dot(features, wq_ref[m // POOLS, m % POOLS])
        sums += own_ref[m, REQ : 3 * REQ, :].astype(F32) + other_ref[m, REQ : 3 * REQ, :].astype(F32)
        extra += own_ref[m, 3 * REQ :, :].astype(F32) + other_ref[m, 3 * REQ :, :].astype(F32)
    row = extra[0:1] + extra[1:2]
    eye = iota((REQ, HD), 0) == iota((REQ, HD), 1)
    squares = jnp.sum(jnp.where(eye, row, 0.0), axis=1, keepdims=True)
    high = squares.astype(BF).astype(F32)
    tail = jnp.where(iota((REQ, HD), 1) < HD // 2, high, squares - high)
    message = jnp.concatenate([q, sums[:REQ], sums[REQ:], tail], axis=1).astype(BF)
    for m in range(POOLS * INSTS):
        out_ref[m] = message


def attend_kernel(got_ref, keys_ref, values_ref, pick_ref, cos_ref, sin_ref, span_ref, out_ref, *, width):
    got = got_ref[...].reshape(POOLS * INSTS * REQ, 4 * HD)
    mine = dot(pick_ref[...], got)
    q, k, v, s = (mine[:, n * HD : (n + 1) * HD] for n in range(4))
    squares = s[:, 0:1] + s[:, HD // 2 : HD // 2 + 1]
    root = jnp.sqrt(squares / width + epsilon)

    def rotate(t):
        return t * cos_ref[...] + pltpu.roll(t, HD // 2, 1) * sin_ref[...]

    q = rotate(q / root).astype(BF)
    k = rotate(k / root).astype(BF)
    v = (v / root).astype(BF)
    keys = keys_ref[...].reshape(REQ * HD, HD)
    values = values_ref[...].reshape(REQ * HD, HD)
    every = lax.dot_general(q, keys, (((1,), (1,)), ((), ())), preferred_element_type=F32)
    request = iota((8, HD), 0)
    rows = []
    for group in range(REQ // 8):
        block = jnp.zeros((8, HD), F32)
        for n in range(8):
            r = group * 8 + n
            block = jnp.where(request == n, every[group * 8 : group * 8 + 8, r * HD : (r + 1) * HD], block)
        rows.append(block)
    factor = HD ** (-0.5)
    scores = jnp.concatenate(rows, axis=0) * factor
    own_score = jnp.sum(q.astype(F32) * k.astype(F32), axis=1, keepdims=True) * factor
    visible = iota((REQ, HD), 1).astype(F32) < span_ref[...]
    scores = jnp.where(visible, scores, -jnp.inf)
    peak = jnp.maximum(jnp.max(scores, axis=1, keepdims=True), own_score)
    exps = jnp.exp(scores - peak)
    own_exp = jnp.exp(own_score - peak)
    total = jnp.sum(exps, axis=1, keepdims=True) + own_exp
    weights = exps / total
    own_weight = (own_exp / total).astype(BF).astype(F32)
    request = iota((REQ, HD), 0)
    spread = jnp.concatenate([jnp.where(request == r, weights, 0.0).astype(BF) for r in range(REQ)], axis=1)
    mixed = (dot(spread, values) + own_weight * v.astype(F32)).astype(BF)
    for m in range(POOLS * INSTS * CORES):
        out_ref[m] = mixed


def output_kernel(got_ref, back_ref, own_ref, other_ref, out_ref):
    core = lax.axis_index("core")
    back = back_ref[...]
    seats = POOLS * INSTS * REQ
    mine = dot(back, got_ref[:, core].reshape(seats, HD)).astype(BF)
    buddy = dot(back, got_ref[:, 1 - core].reshape(seats, HD)).astype(BF)
    result = (dot(mine, own_ref[...]) + dot(buddy, other_ref[...])).astype(BF)
    for m in range(RING):
        out_ref[m] = result[:, m * HD : (m + 1) * HD]


def sum_kernel(got_ref, out_ref):
    total = got_ref[0].astype(F32)
    for m in range(1, RING):
        total += got_ref[m].astype(F32)
    out_ref[0] = total.astype(BF)


def in_hbm(*arrays):
    return [pltpu.with_memory_space_constraint(a, pltpu.HBM) for a in arrays]


def call(kernel, shapes, specs, flops, moved, scratch=(), limit=24):
    one = not isinstance(shapes, list)
    return pl.pallas_call(
        kernel,
        out_shape=shapes if one else tuple(shapes),
        in_specs=specs,
        out_specs=VMEM if one else tuple(VMEM for _ in shapes),
        scratch_shapes=list(scratch),
        cost_estimate=pl.CostEstimate(flops=flops, bytes_accessed=moved, transcendentals=0),
        compiler_params=pltpu.CompilerParams(vmem_limit_bytes=limit << 20),
    )


def shape(*dims, dtype=BF):
    return jax.ShapeDtypeStruct(dims, dtype)


def shards(
    hidden_states,
    norm_gain,
    query_weight,
    key_weight,
    value_weight,
    output_weight,
    key_cache,
    value_cache,
    lengths,
    offload,
    host_instance,
    cache_slot,
):
    width = query_weight.shape[0]
    seats = POOLS * INSTS * REQ

    buddy_weight = swap_core(output_weight)
    message = call(
        features_kernel,
        shape(RING, 3 * REQ + 16, HD),
        [HBM] * 4,
        1 << 23,
        1 << 20,
        [
            pltpu.VMEM((1, REQ, HD), BF),
            pltpu.VMEM((1, HD), BF),
            pltpu.VMEM(key_weight.shape, BF),
            pltpu.VMEM(value_weight.shape, BF),
            pltpu.SemaphoreType.DMA((4,)),
        ],
    )(*in_hbm(hidden_states, norm_gain.reshape(1, HD), key_weight, value_weight))
    message, lengths = lax.optimization_barrier((message, lengths))
    got = ring_exchange(message)
    table = pltpu.VMEM(lengths.shape, I32)
    early = call(
        early_kernel,
        [
            shape(REQ, HD, HD),
            shape(ZS, POOLS, CORES * HD, HD),
            shape(REQ, seats),
            shape(REQ, seats),
            shape(REQ, HD, dtype=F32),
            shape(REQ, HD, dtype=F32),
            shape(REQ, HD, dtype=F32),
        ],
        [HBM] * 6,
        1 << 22,
        1 << 22,
        [table] * 4 + [pltpu.SemaphoreType.DMA((4 + 2 * POOLS + 1,))],
    )(
        *in_hbm(
            lengths,
            offload,
            host_instance,
            cache_slot,
            key_cache,
            query_weight.reshape(POOLS, ZS, YS, CORES, HD, HD),
        )
    )
    got, early, value_cache = lax.optimization_barrier((got, early, value_cache))
    keys, wq, pick, back, cos, sin, span = early
    other = swap_core(got)
    late = call(
        late_kernel,
        [shape(REQ, HD, HD), shape(HD, RING * HD), shape(HD, RING * HD)],
        [HBM] * 3,
        0,
        1 << 22,
        [pltpu.SemaphoreType.DMA((1 + 2 * RING,))],
    )(*in_hbm(value_cache, output_weight, buddy_weight))
    other, (values, keep, taken) = lax.optimization_barrier((other, late))
    message = call(query_kernel, shape(POOLS * INSTS, REQ, 4 * HD), [VMEM] * 3, 1 << 25, 1 << 22)(got, other, wq)
    got = lax.all_to_all(message, ("pool", "inst"), 0, 0, tiled=True)
    message = call(
        functools.partial(attend_kernel, width=width), shape(POOLS * INSTS * CORES, REQ, HD), [VMEM] * 7, 1 << 26, 1 << 22
    )(got, keys, values, pick, cos, sin, span)
    got = lax.all_to_all(message, ("pool", "inst", "core"), 0, 0, tiled=True)
    message = call(output_kernel, shape(RING, REQ, HD), [VMEM] * 4, 1 << 25, 1 << 22)(
        got.reshape(POOLS * INSTS, CORES, REQ, HD), back, keep, taken
    )
    got = ring_exchange(message)
    return call(sum_kernel, shape(1, REQ, HD), [VMEM], 1 << 17, 1 << 18)(got)


def solution(mesh):
    finer = Mesh(mesh.devices.reshape(SIZES), AXES)
    in_specs = (
        P("inst", None, ("pool",) + TP),
        P(("pool",) + TP),
        P(None, TP),
        P(("pool",) + TP, None),
        P(("pool",) + TP, None),
        P(TP, None),
        P("pool", "inst", None, None, None),
        P("pool", "inst", None, None, None),
        P(),
        P(),
        P(),
        P(),
    )
    out_specs = P("inst", None, ("pool",) + TP)
    return jax.shard_map(shards, mesh=finer, in_specs=in_specs, out_specs=out_specs, check_vma=False)
```

```python
import functools

import jax
import jax.numpy as jnp
from jax import lax
from jax.experimental import pallas as pl
from jax.experimental.pallas import tpu as pltpu
from jax.sharding import Mesh
from jax.sharding import PartitionSpec as P

HD = 128
HEADS = 4
REQ = 32
POOLS, INSTS, ZS, YS, CORES = 2, 4, 8, 2, 2
RING = ZS * POOLS
EXTRA = 8
epsilon = 1e-05
rope_base = 500000.0
AXES = ("pool", "inst", "z", "yh", "core")
SIZES = (POOLS, INSTS, ZS, YS, CORES)
TP = ("z", "yh", "core")
BF = jnp.bfloat16
F32 = jnp.float32
I32 = jnp.int32
VMEM = pl.BlockSpec(memory_space=pltpu.VMEM)
HBM = pl.BlockSpec(memory_space=pltpu.HBM)


def device_number(p, i, z, y, c):
    return (((p * INSTS + i) * ZS + z) * YS + y) * CORES + c


RINGS = [
    [device_number(p, i, z, p ^ s, c) for z in range(ZS) for p in range(POOLS)]
    for s in range(2)
    for i in range(INSTS)
    for c in range(CORES)
]


def ring_exchange(x):
    return lax.all_to_all(x, AXES, 0, 0, axis_index_groups=RINGS, tiled=True)


def swap_core(x):
    return lax.ppermute(x, "core", [(0, 1), (1, 0)])


def iota(shape, axis):
    return lax.broadcasted_iota(I32, shape, axis)


def dot(a, b):
    return jnp.dot(a, b, preferred_element_type=F32)


def split(x):
    high = x.astype(BF)
    return high, (x - high.astype(F32)).astype(BF)


def start_copies(pairs, sems):
    copies = [pltpu.make_async_copy(a, b, sems.at[n]) for n, (a, b) in enumerate(pairs)]
    for copy in copies:
        copy.start()
    return copies


def head_lanes(z):
    return pl.ds(pl.multiple_of((z // (ZS // HEADS)) * HD, HD), HD)


def two_rows(row):
    high = row.astype(BF).astype(F32)
    at = iota((EXTRA, HD), 0)
    return jnp.where(at == 0, high, jnp.where(at == 1, row - high, 0.0)).astype(BF)


def features_kernel(
    x_hbm, gain_hbm, wk_hbm, wv_hbm,
    scaled_out, extra_out, keep_out, give_out,
    x_ref, gain_ref, wk_ref, wv_ref, sems,
):
    pairs = ((x_hbm, x_ref), (gain_hbm, gain_ref), (wk_hbm, wk_ref), (wv_hbm, wv_ref))
    for copy in start_copies(pairs, sems):
        copy.wait()
    x = x_ref[0].astype(F32)
    scaled = (x * gain_ref[...].astype(F32)).astype(BF)
    squares = jnp.sum(x * x, axis=1, keepdims=True)
    place = iota((REQ, HD), 0) + lax.axis_index("inst") * REQ == iota((REQ, HD), 1)
    scaled_out[...] = scaled
    extra_out[...] = two_rows(jnp.sum(jnp.where(place, squares, 0.0), axis=0, keepdims=True))
    k = dot(scaled, wk_ref[...])
    v = dot(scaled, wv_ref[...])
    first = lax.axis_index("core") == 0
    keep_out[...] = jnp.where(first, k, v).astype(BF)
    give_out[...] = jnp.where(first, v, k).astype(BF)


def message_kernel(scaled_ref, extra_ref, keep_ref, taken_ref, out_ref):
    terms = (keep_ref[...].astype(F32) + taken_ref[...].astype(F32)).astype(BF)
    for m in range(RING):
        n = (m // POOLS) // (ZS // HEADS)
        out_ref[m, 0:REQ, :] = scaled_ref[...]
        out_ref[m, REQ : 2 * REQ, :] = terms[:, n * HD : (n + 1) * HD]
        out_ref[m, 2 * REQ :, :] = extra_ref[...]


def output_columns(source, out):
    core = lax.axis_index("core")
    side = lax.axis_index("pool") ^ lax.axis_index("yh")
    pairs = []
    for m in range(RING):
        z, p = m // POOLS, m % POOLS
        block = ((p * ZS + z) * YS + (p ^ side)) * CORES + core
        lanes = pl.ds(pl.multiple_of(block * HD, HD), HD)
        pairs.append((source.at[:, lanes], out.at[:, pl.ds(m * HD, HD)]))
    return pairs


def early_kernel(
    lengths_hbm, offload_hbm, host_hbm, slot_hbm, keys_hbm, values_hbm, wo_hbm,
    keys_out, values_out, wo_out, pick_ref, back_ref, cos_ref, sin_ref, span_ref,
    lengths_ref, offload_ref, host_ref, slot_ref, sems,
):
    pool, inst, z = lax.axis_index("pool"), lax.axis_index("inst"), lax.axis_index("z")
    pairs = [(lengths_hbm, lengths_ref), (offload_hbm, offload_ref), (host_hbm, host_ref), (slot_hbm, slot_ref)]
    small = len(pairs)
    pairs.append((keys_hbm.at[0, 0, :, :, head_lanes(z)], keys_out))
    pairs.append((values_hbm.at[0, 0, :, :, head_lanes(z)], values_out))
    copies = start_copies(pairs + output_columns(wo_hbm, wo_out), sems)
    for copy in copies[:small]:
        copy.wait()
    home = iota((INSTS, REQ), 0) * REQ + iota((INSTS, REQ), 1)
    away = INSTS * REQ + host_ref[...] * REQ + slot_ref[...]
    seat = jnp.where(offload_ref[...] == 1, away, home)
    spans = lengths_ref[...].astype(F32)
    here = iota((REQ, REQ), 0) + (pool * INSTS + inst) * REQ
    square = iota((REQ, REQ), 0) == iota((REQ, REQ), 1)
    pick = jnp.zeros((REQ, POOLS * INSTS * REQ), F32)
    span = jnp.zeros((REQ, 1), F32)
    column = jnp.zeros((REQ, 1), F32)
    for i in range(INSTS):
        sits = seat[i : i + 1, :] == here
        wide = iota((REQ, POOLS * INSTS * REQ), 1) % (INSTS * REQ)
        place = (wide == iota(wide.shape, 0) + i * REQ).astype(F32).astype(BF)
        pick += dot(sits.astype(F32).astype(BF), place)
        span += jnp.sum(jnp.where(sits, spans[i : i + 1, :], 0.0), axis=1, keepdims=True)
        turned = jnp.sum(jnp.where(square, seat[i : i + 1, :].astype(F32), 0.0), axis=1, keepdims=True)
        column += jnp.where(inst == i, turned, 0.0)
    pick_ref[...] = pick.astype(BF)
    seats = iota((REQ, POOLS * INSTS * REQ), 1).astype(F32)
    back_ref[...] = (column == seats).astype(F32).astype(BF)
    half = HD // 2
    lanes = iota((REQ, HD), 1)
    frequency = jnp.exp((lanes % half).astype(F32) * (-2.0 / HD * 13.122363377404328))
    angles = span * frequency
    cos_ref[...] = jnp.cos(angles)
    sin_ref[...] = jnp.where(lanes < half, -jnp.sin(angles), jnp.sin(angles))
    span_ref[...] = jnp.broadcast_to(span, (REQ, HD))
    for copy in copies[small:]:
        copy.wait()


def late_kernel(wq_hbm, wo_hbm, wq_out, wo_out, sems):
    core = lax.axis_index("core")
    side = lax.axis_index("pool") ^ lax.axis_index("yh")
    pairs = []
    for p in range(POOLS):
        for n, c in enumerate((core, 1 - core)):
            pairs.append((wq_hbm.at[p, :, p ^ side, c], wq_out.at[:, p, pl.ds(n * HD, HD), :]))
    for copy in start_copies(pairs + output_columns(wo_hbm, wo_out), sems):
        copy.wait()


def query_kernel(own_ref, other_ref, wq_ref, out_ref):
    q = jnp.zeros((REQ, HD), F32)
    own = jnp.zeros((REQ, HD), F32)
    other = jnp.zeros((REQ, HD), F32)
    extra = jnp.zeros((EXTRA, HD), F32)
    for m in range(RING):
        features = jnp.concatenate([own_ref[m, 0:REQ, :], other_ref[m, 0:REQ, :]], axis=1)
        q += dot(features, wq_ref[m // POOLS, m % POOLS])
        own += own_ref[m, REQ : 2 * REQ, :].astype(F32)
        other += other_ref[m, REQ : 2 * REQ, :].astype(F32)
        extra += own_ref[m, 2 * REQ :, :].astype(F32) + other_ref[m, 2 * REQ :, :].astype(F32)
    first = lax.axis_index("core") == 0
    k, v = jnp.where(first, own, other), jnp.where(first, other, own)
    rest = two_rows(extra[0:1] + extra[1:2])
    for m in range(POOLS * INSTS):
        for n, part in enumerate((q, k, v)):
            out_ref[m, n * REQ : (n + 1) * REQ, :] = part.astype(BF)
        out_ref[m, 3 * REQ :, :] = rest


def attend_kernel(got_ref, keys_ref, values_ref, pick_ref, cos_ref, sin_ref, span_ref, out_ref, *, width):
    pick = pick_ref[...]
    q, k, v = (dot(pick, got_ref[:, n * REQ : (n + 1) * REQ, :].reshape(pick.shape[1], HD)) for n in range(3))
    rest = jnp.zeros((EXTRA, HD), F32)
    for m in range(POOLS * INSTS):
        rest += got_ref[m, 3 * REQ :, :].astype(F32)
    squares = jnp.sum(pick[:, :HD].astype(F32) * (rest[0:1] + rest[1:2]), axis=1, keepdims=True)
    root = jnp.sqrt(squares / width + epsilon)

    def rotate(t):
        return t * cos_ref[...] + pltpu.roll(t, HD // 2, 1) * sin_ref[...]

    q = rotate(q / root).astype(BF)
    k = rotate(k / root).astype(BF)
    v = (v / root).astype(BF)
    keys = keys_ref[...].reshape(REQ * HD, HD)
    values = values_ref[...].reshape(REQ * HD, HD)
    every = lax.dot_general(q, keys, (((1,), (1,)), ((), ())), preferred_element_type=F32)
    request = iota((8, HD), 0)
    rows = []
    for group in range(REQ // 8):
        block = jnp.zeros((8, HD), F32)
        for n in range(8):
            r = group * 8 + n
            block = jnp.where(request == n, every[group * 8 : group * 8 + 8, r * HD : (r + 1) * HD], block)
        rows.append(block)
    factor = HD ** (-0.5)
    scores = jnp.concatenate(rows, axis=0) * factor
    own_score = jnp.sum(q.astype(F32) * k.astype(F32), axis=1, keepdims=True) * factor
    visible = iota((REQ, HD), 1).astype(F32) < span_ref[...]
    scores = jnp.where(visible, scores, -jnp.inf)
    peak = jnp.maximum(jnp.max(scores, axis=1, keepdims=True), own_score)
    exps = jnp.exp(scores - peak)
    own_exp = jnp.exp(own_score - peak)
    total = jnp.sum(exps, axis=1, keepdims=True) + own_exp
    weights = exps / total
    own_weight = (own_exp / total).astype(BF).astype(F32)
    request = iota((REQ, HD), 0)
    spread = jnp.concatenate([jnp.where(request == r, weights, 0.0).astype(BF) for r in range(REQ)], axis=1)
    mixed = (dot(spread, values) + own_weight * v.astype(F32)).astype(BF)
    for m in range(POOLS * INSTS * CORES):
        out_ref[m] = mixed


def output_kernel(got_ref, back_ref, own_ref, other_ref, out_ref):
    core = lax.axis_index("core")
    back = back_ref[...]
    seats = POOLS * INSTS * REQ
    mine = dot(back, got_ref[:, core].reshape(seats, HD)).astype(BF)
    buddy = dot(back, got_ref[:, 1 - core].reshape(seats, HD)).astype(BF)
    result = (dot(mine, own_ref[...]) + dot(buddy, other_ref[...])).astype(BF)
    for m in range(RING):
        out_ref[m] = result[:, m * HD : (m + 1) * HD]


def sum_kernel(got_ref, out_ref):
    total = got_ref[0].astype(F32)
    for m in range(1, RING):
        total += got_ref[m].astype(F32)
    out_ref[0] = total.astype(BF)


def in_hbm(*arrays):
    return [pltpu.with_memory_space_constraint(a, pltpu.HBM) for a in arrays]


def call(kernel, shapes, specs, flops, moved, scratch=(), limit=24):
    one = not isinstance(shapes, list)
    return pl.pallas_call(
        kernel,
        out_shape=shapes if one else tuple(shapes),
        in_specs=specs,
        out_specs=VMEM if one else tuple(VMEM for _ in shapes),
        scratch_shapes=list(scratch),
        cost_estimate=pl.CostEstimate(flops=flops, bytes_accessed=moved, transcendentals=0),
        compiler_params=pltpu.CompilerParams(vmem_limit_bytes=limit << 20),
    )


def shape(*dims, dtype=BF):
    return jax.ShapeDtypeStruct(dims, dtype)


def shards(
    hidden_states,
    norm_gain,
    query_weight,
    key_weight,
    value_weight,
    output_weight,
    key_cache,
    value_cache,
    lengths,
    offload,
    host_instance,
    cache_slot,
):
    width = query_weight.shape[0]
    seats = POOLS * INSTS * REQ

    scaled, extra, keep, give = call(
        features_kernel,
        [shape(REQ, HD), shape(EXTRA, HD), shape(REQ, HEADS * HD), shape(REQ, HEADS * HD)],
        [HBM] * 4,
        1 << 23,
        1 << 20,
        [
            pltpu.VMEM((1, REQ, HD), BF),
            pltpu.VMEM((1, HD), BF),
            pltpu.VMEM(key_weight.shape, BF),
            pltpu.VMEM(value_weight.shape, BF),
            pltpu.SemaphoreType.DMA((4,)),
        ],
    )(*in_hbm(hidden_states, norm_gain.reshape(1, HD), key_weight, value_weight))
    message = call(message_kernel, shape(RING, 2 * REQ + EXTRA, HD), [VMEM] * 4, 1 << 14, 1 << 19)(
        scaled, extra, keep, swap_core(give)
    )
    message, lengths, output_weight = lax.optimization_barrier((message, lengths, output_weight))
    buddy_weight = swap_core(output_weight)
    got = ring_exchange(message)
    table = pltpu.VMEM(lengths.shape, I32)
    early = call(
        early_kernel,
        [
            shape(REQ, HD, HD),
            shape(REQ, HD, HD),
            shape(HD, RING * HD),
            shape(REQ, seats),
            shape(REQ, seats),
            shape(REQ, HD, dtype=F32),
            shape(REQ, HD, dtype=F32),
            shape(REQ, HD, dtype=F32),
        ],
        [HBM] * 7,
        1 << 22,
        1 << 22,
        [table] * 4 + [pltpu.SemaphoreType.DMA((6 + RING,))],
    )(*in_hbm(lengths, offload, host_instance, cache_slot, key_cache, value_cache, output_weight))
    got, early, query_weight = lax.optimization_barrier((got, early, query_weight))
    keys, values, keep, pick, back, cos, sin, span = early
    other = swap_core(got)
    late = call(
        late_kernel,
        [shape(ZS, POOLS, CORES * HD, HD), shape(HD, RING * HD)],
        [HBM] * 2,
        0,
        1 << 22,
        [pltpu.SemaphoreType.DMA((2 * POOLS + RING,))],
    )(*in_hbm(query_weight.reshape(POOLS, ZS, YS, CORES, HD, HD), buddy_weight))
    other, (wq, taken) = lax.optimization_barrier((other, late))
    message = call(query_kernel, shape(POOLS * INSTS, 3 * REQ + EXTRA, HD), [VMEM] * 3, 1 << 25, 1 << 22)(got, other, wq)
    got = lax.all_to_all(message, ("pool", "inst"), 0, 0, tiled=True)
    message = call(
        functools.partial(attend_kernel, width=width), shape(POOLS * INSTS * CORES, REQ, HD), [VMEM] * 7, 1 << 26, 1 << 22
    )(got, keys, values, pick, cos, sin, span)
    got = lax.all_to_all(message, ("pool", "inst", "core"), 0, 0, tiled=True)
    message = call(output_kernel, shape(RING, REQ, HD), [VMEM] * 4, 1 << 25, 1 << 22)(
        got.reshape(POOLS * INSTS, CORES, REQ, HD), back, keep, taken
    )
    got = ring_exchange(message)
    return call(sum_kernel, shape(1, REQ, HD), [VMEM], 1 << 17, 1 << 18)(got)


def solution(mesh):
    finer = Mesh(mesh.devices.reshape(SIZES), AXES)
    in_specs = (
        P("inst", None, ("pool",) + TP),
        P(("pool",) + TP),
        P(None, TP),
        P(("pool",) + TP, None),
        P(("pool",) + TP, None),
        P(TP, None),
        P("pool", "inst", None, None, None),
        P("pool", "inst", None, None, None),
        P(),
        P(),
        P(),
        P(),
    )
    out_specs = P("inst", None, ("pool",) + TP)
    return jax.shard_map(shards, mesh=finer, in_specs=in_specs, out_specs=out_specs, check_vma=False)
```

```python
import functools

import jax
import jax.numpy as jnp
from jax import lax
from jax.experimental import pallas as pl
from jax.experimental.pallas import tpu as pltpu
from jax.sharding import Mesh
from jax.sharding import PartitionSpec as P

HD = 128
HEADS = 4
REQ = 32
POOLS, INSTS, ZS, YS, CORES = 2, 4, 8, 2, 2
RING = ZS * POOLS
EXTRA = 8
epsilon = 1e-05
rope_base = 500000.0
AXES = ("pool", "inst", "z", "yh", "core")
SIZES = (POOLS, INSTS, ZS, YS, CORES)
TP = ("z", "yh", "core")
BF = jnp.bfloat16
F32 = jnp.float32
I32 = jnp.int32
VMEM = pl.BlockSpec(memory_space=pltpu.VMEM)
HBM = pl.BlockSpec(memory_space=pltpu.HBM)


def device_number(p, i, z, y, c):
    return (((p * INSTS + i) * ZS + z) * YS + y) * CORES + c


PLACES = [((z + 5) % ZS, 1 - y) for z in range(ZS) for y in range(YS)]
RINGS = [
    [device_number(y ^ s, i, z, y, c) for z, y in PLACES]
    for s in range(2)
    for i in range(INSTS)
    for c in range(CORES)
]


FIRST = 2
HEADS_ALIKE = [(z, y, c) for z in range(ZS) for y in range(YS) for c in range(CORES)]
TURNS = [(a, (i + FIRST) % INSTS) for a in range(POOLS) for i in range(INSTS)]
HOSTS = [[device_number(a ^ y, i, z, y, c) for a, i in TURNS] for z, y, c in HEADS_ALIKE]
CHIPS = [
    [device_number(a ^ y, i, z, y, c) for a, i in TURNS for c in range(CORES)]
    for z in range(ZS)
    for y in range(YS)
]


def turn(inst):
    return (inst + (INSTS - FIRST)) % INSTS


def exchange(x, groups):
    return lax.all_to_all(x, AXES, 0, 0, axis_index_groups=groups, tiled=True)


def swap_core(x):
    return lax.ppermute(x, "core", [(0, 1), (1, 0)])


def iota(shape, axis):
    return lax.broadcasted_iota(I32, shape, axis)


def dot(a, b):
    return jnp.dot(a, b, preferred_element_type=F32)


def split(x):
    high = x.astype(BF)
    return high, (x - high.astype(F32)).astype(BF)


def start_copies(pairs, sems):
    copies = [pltpu.make_async_copy(a, b, sems.at[n]) for n, (a, b) in enumerate(pairs)]
    for copy in copies:
        copy.start()
    return copies


def head_lanes(z):
    return pl.ds(pl.multiple_of((z // (ZS // HEADS)) * HD, HD), HD)


def two_rows(row):
    high = row.astype(BF).astype(F32)
    at = iota((EXTRA, HD), 0)
    return jnp.where(at == 0, high, jnp.where(at == 1, row - high, 0.0)).astype(BF)


def features_kernel(
    x_hbm, gain_hbm, wk_hbm, wv_hbm,
    scaled_out, extra_out, keep_out, give_out,
    x_ref, gain_ref, wk_ref, wv_ref, sems,
):
    pairs = ((x_hbm, x_ref), (gain_hbm, gain_ref), (wk_hbm, wk_ref), (wv_hbm, wv_ref))
    for copy in start_copies(pairs, sems):
        copy.wait()
    x = x_ref[0].astype(F32)
    scaled = (x * gain_ref[...].astype(F32)).astype(BF)
    squares = jnp.sum(x * x, axis=1, keepdims=True)
    place = iota((REQ, HD), 0) + turn(lax.axis_index("inst")) * REQ == iota((REQ, HD), 1)
    scaled_out[...] = scaled
    extra_out[...] = two_rows(jnp.sum(jnp.where(place, squares, 0.0), axis=0, keepdims=True))
    k = dot(scaled, wk_ref[...])
    v = dot(scaled, wv_ref[...])
    first = lax.axis_index("core") == 0
    keep_out[...] = jnp.where(first, k, v).astype(BF)
    give_out[...] = jnp.where(first, v, k).astype(BF)


def message_kernel(scaled_ref, extra_ref, keep_ref, taken_ref, out_ref):
    terms = (keep_ref[...].astype(F32) + taken_ref[...].astype(F32)).astype(BF)
    for m, (z, _) in enumerate(PLACES):
        n = z // (ZS // HEADS)
        out_ref[m, 0:REQ, :] = scaled_ref[...]
        out_ref[m, REQ : 2 * REQ, :] = terms[:, n * HD : (n + 1) * HD]
        out_ref[m, 2 * REQ :, :] = extra_ref[...]


def output_columns(source, out):
    core = lax.axis_index("core")
    side = lax.axis_index("pool") ^ lax.axis_index("yh")
    pairs = []
    for m, (z, y) in enumerate(PLACES):
        block = (((y ^ side) * ZS + z) * YS + y) * CORES + core
        lanes = pl.ds(pl.multiple_of(block * HD, HD), HD)
        pairs.append((source.at[:, lanes], out.at[:, pl.ds(m * HD, HD)]))
    return pairs


def early_kernel(
    lengths_hbm, offload_hbm, host_hbm, slot_hbm, keys_hbm, values_hbm, wo_hbm,
    keys_out, values_out, wo_out, pick_ref, back_ref, cos_ref, sin_ref, span_ref,
    lengths_ref, offload_ref, host_ref, slot_ref, sems,
):
    pool, inst, z = lax.axis_index("pool"), lax.axis_index("inst"), lax.axis_index("z")
    pairs = [(lengths_hbm, lengths_ref), (offload_hbm, offload_ref), (host_hbm, host_ref), (slot_hbm, slot_ref)]
    small = len(pairs)
    pairs.append((keys_hbm.at[0, 0, :, :, head_lanes(z)], keys_out))
    pairs.append((values_hbm.at[0, 0, :, :, head_lanes(z)], values_out))
    copies = start_copies(pairs + output_columns(wo_hbm, wo_out), sems)
    for copy in copies[:small]:
        copy.wait()
    yh = lax.axis_index("yh")
    home = yh * (INSTS * REQ) + turn(iota((INSTS, REQ), 0)) * REQ + iota((INSTS, REQ), 1)
    away = (1 - yh) * (INSTS * REQ) + turn(host_ref[...]) * REQ + slot_ref[...]
    seat = jnp.where(offload_ref[...] == 1, away, home)
    spans = lengths_ref[...].astype(F32)
    here = iota((REQ, REQ), 0) + ((pool ^ yh) * INSTS + turn(inst)) * REQ
    square = iota((REQ, REQ), 0) == iota((REQ, REQ), 1)
    pick = jnp.zeros((REQ, POOLS * INSTS * REQ), F32)
    span = jnp.zeros((REQ, 1), F32)
    column = jnp.zeros((REQ, 1), F32)
    for i in range(INSTS):
        sits = seat[i : i + 1, :] == here
        wide = iota((REQ, POOLS * INSTS * REQ), 1) % (INSTS * REQ)
        place = (wide == iota(wide.shape, 0) + turn(i) * REQ).astype(F32).astype(BF)
        pick += dot(sits.astype(F32).astype(BF), place)
        span += jnp.sum(jnp.where(sits, spans[i : i + 1, :], 0.0), axis=1, keepdims=True)
        turned = jnp.sum(jnp.where(square, seat[i : i + 1, :].astype(F32), 0.0), axis=1, keepdims=True)
        column += jnp.where(inst == i, turned, 0.0)
    pick_ref[...] = pick.astype(BF)
    seats = iota((REQ, POOLS * INSTS * REQ), 1).astype(F32)
    back_ref[...] = (column == seats).astype(F32).astype(BF)
    half = HD // 2
    lanes = iota((REQ, HD), 1)
    frequency = jnp.exp((lanes % half).astype(F32) * (-2.0 / HD * 13.122363377404328))
    angles = span * frequency
    cos_ref[...] = jnp.cos(angles)
    sin_ref[...] = jnp.where(lanes < half, -jnp.sin(angles), jnp.sin(angles))
    span_ref[...] = jnp.broadcast_to(span, (REQ, HD))
    for copy in copies[small:]:
        copy.wait()


def late_kernel(wq_hbm, wo_hbm, wq_out, wo_out, sems):
    core = lax.axis_index("core")
    side = lax.axis_index("pool") ^ lax.axis_index("yh")
    pairs = []
    for y in range(YS):
        for n, c in enumerate((core, 1 - core)):
            pairs.append((wq_hbm.at[y ^ side, :, y, c], wq_out.at[:, y, pl.ds(n * HD, HD), :]))
    for copy in start_copies(pairs + output_columns(wo_hbm, wo_out), sems):
        copy.wait()


def query_kernel(own_ref, other_ref, wq_ref, out_ref):
    q = jnp.zeros((REQ, HD), F32)
    own = jnp.zeros((REQ, HD), F32)
    other = jnp.zeros((REQ, HD), F32)
    extra = jnp.zeros((EXTRA, HD), F32)
    for m, place in enumerate(PLACES):
        features = jnp.concatenate([own_ref[m, 0:REQ, :], other_ref[m, 0:REQ, :]], axis=1)
        q += dot(features, wq_ref[place])
        own += own_ref[m, REQ : 2 * REQ, :].astype(F32)
        other += other_ref[m, REQ : 2 * REQ, :].astype(F32)
        extra += own_ref[m, 2 * REQ :, :].astype(F32) + other_ref[m, 2 * REQ :, :].astype(F32)
    first = lax.axis_index("core") == 0
    k, v = jnp.where(first, own, other), jnp.where(first, other, own)
    rest = two_rows(extra[0:1] + extra[1:2])
    for m in range(POOLS * INSTS):
        for n, part in enumerate((q, k, v)):
            out_ref[m, n * REQ : (n + 1) * REQ, :] = part.astype(BF)
        out_ref[m, 3 * REQ :, :] = rest


def attend_kernel(got_ref, keys_ref, values_ref, pick_ref, cos_ref, sin_ref, span_ref, out_ref, *, width):
    pick = pick_ref[...]
    q, k, v = (dot(pick, got_ref[:, n * REQ : (n + 1) * REQ, :].reshape(pick.shape[1], HD)) for n in range(3))
    rest = jnp.zeros((EXTRA, HD), F32)
    for m in range(POOLS * INSTS):
        rest += got_ref[m, 3 * REQ :, :].astype(F32)
    squares = jnp.sum(pick[:, :HD].astype(F32) * (rest[0:1] + rest[1:2]), axis=1, keepdims=True)
    root = jnp.sqrt(squares / width + epsilon)

    def rotate(t):
        return t * cos_ref[...] + pltpu.roll(t, HD // 2, 1) * sin_ref[...]

    q = rotate(q / root).astype(BF)
    k = rotate(k / root).astype(BF)
    v = (v / root).astype(BF)
    keys = keys_ref[...].reshape(REQ * HD, HD)
    values = values_ref[...].reshape(REQ * HD, HD)
    every = lax.dot_general(q, keys, (((1,), (1,)), ((), ())), preferred_element_type=F32)
    request = iota((8, HD), 0)
    rows = []
    for group in range(REQ // 8):
        block = jnp.zeros((8, HD), F32)
        for n in range(8):
            r = group * 8 + n
            block = jnp.where(request == n, every[group * 8 : group * 8 + 8, r * HD : (r + 1) * HD], block)
        rows.append(block)
    factor = HD ** (-0.5)
    scores = jnp.concatenate(rows, axis=0) * factor
    own_score = jnp.sum(q.astype(F32) * k.astype(F32), axis=1, keepdims=True) * factor
    visible = iota((REQ, HD), 1).astype(F32) < span_ref[...]
    scores = jnp.where(visible, scores, -jnp.inf)
    peak = jnp.maximum(jnp.max(scores, axis=1, keepdims=True), own_score)
    exps = jnp.exp(scores - peak)
    own_exp = jnp.exp(own_score - peak)
    total = jnp.sum(exps, axis=1, keepdims=True) + own_exp
    weights = exps / total
    own_weight = (own_exp / total).astype(BF).astype(F32)
    request = iota((REQ, HD), 0)
    spread = jnp.concatenate([jnp.where(request == r, weights, 0.0).astype(BF) for r in range(REQ)], axis=1)
    mixed = (dot(spread, values) + own_weight * v.astype(F32)).astype(BF)
    for m in range(POOLS * INSTS * CORES):
        out_ref[m] = mixed


def output_kernel(got_ref, back_ref, own_ref, other_ref, out_ref):
    core = lax.axis_index("core")
    back = back_ref[...]
    seats = POOLS * INSTS * REQ
    mine = dot(back, got_ref[:, core].reshape(seats, HD)).astype(BF)
    buddy = dot(back, got_ref[:, 1 - core].reshape(seats, HD)).astype(BF)
    result = (dot(mine, own_ref[...]) + dot(buddy, other_ref[...])).astype(BF)
    for m in range(RING):
        out_ref[m] = result[:, m * HD : (m + 1) * HD]


def sum_kernel(got_ref, out_ref):
    total = got_ref[0].astype(F32)
    for m in range(1, RING):
        total += got_ref[m].astype(F32)
    out_ref[0] = total.astype(BF)


def in_hbm(*arrays):
    return [pltpu.with_memory_space_constraint(a, pltpu.HBM) for a in arrays]


def call(kernel, shapes, specs, flops, moved, scratch=(), limit=24):
    one = not isinstance(shapes, list)
    return pl.pallas_call(
        kernel,
        out_shape=shapes if one else tuple(shapes),
        in_specs=specs,
        out_specs=VMEM if one else tuple(VMEM for _ in shapes),
        scratch_shapes=list(scratch),
        cost_estimate=pl.CostEstimate(flops=flops, bytes_accessed=moved, transcendentals=0),
        compiler_params=pltpu.CompilerParams(vmem_limit_bytes=limit << 20),
    )


def shape(*dims, dtype=BF):
    return jax.ShapeDtypeStruct(dims, dtype)


def shards(
    hidden_states,
    norm_gain,
    query_weight,
    key_weight,
    value_weight,
    output_weight,
    key_cache,
    value_cache,
    lengths,
    offload,
    host_instance,
    cache_slot,
):
    width = query_weight.shape[0]
    seats = POOLS * INSTS * REQ

    scaled, extra, keep, give = call(
        features_kernel,
        [shape(REQ, HD), shape(EXTRA, HD), shape(REQ, HEADS * HD), shape(REQ, HEADS * HD)],
        [HBM] * 4,
        1 << 23,
        1 << 20,
        [
            pltpu.VMEM((1, REQ, HD), BF),
            pltpu.VMEM((1, HD), BF),
            pltpu.VMEM(key_weight.shape, BF),
            pltpu.VMEM(value_weight.shape, BF),
            pltpu.SemaphoreType.DMA((4,)),
        ],
    )(*in_hbm(hidden_states, norm_gain.reshape(1, HD), key_weight, value_weight))
    message = call(message_kernel, shape(RING, 2 * REQ + EXTRA, HD), [VMEM] * 4, 1 << 14, 1 << 19)(
        scaled, extra, keep, swap_core(give)
    )
    message, lengths, output_weight = lax.optimization_barrier((message, lengths, output_weight))
    buddy_weight = swap_core(output_weight)
    got = exchange(message, RINGS)
    table = pltpu.VMEM(lengths.shape, I32)
    early = call(
        early_kernel,
        [
            shape(REQ, HD, HD),
            shape(REQ, HD, HD),
            shape(HD, RING * HD),
            shape(REQ, seats),
            shape(REQ, seats),
            shape(REQ, HD, dtype=F32),
            shape(REQ, HD, dtype=F32),
            shape(REQ, HD, dtype=F32),
        ],
        [HBM] * 7,
        1 << 22,
        1 << 22,
        [table] * 4 + [pltpu.SemaphoreType.DMA((6 + RING,))],
    )(*in_hbm(lengths, offload, host_instance, cache_slot, key_cache, value_cache, output_weight))
    got, early, query_weight = lax.optimization_barrier((got, early, query_weight))
    keys, values, keep, pick, back, cos, sin, span = early
    other = swap_core(got)
    late = call(
        late_kernel,
        [shape(ZS, YS, CORES * HD, HD), shape(HD, RING * HD)],
        [HBM] * 2,
        0,
        1 << 22,
        [pltpu.SemaphoreType.DMA((2 * YS + RING,))],
    )(*in_hbm(query_weight.reshape(POOLS, ZS, YS, CORES, HD, HD), buddy_weight))
    other, (wq, taken) = lax.optimization_barrier((other, late))
    message = call(query_kernel, shape(POOLS * INSTS, 3 * REQ + EXTRA, HD), [VMEM] * 3, 1 << 25, 1 << 22)(got, other, wq)
    got = exchange(message, HOSTS)
    message = call(
        functools.partial(attend_kernel, width=width), shape(POOLS * INSTS * CORES, REQ, HD), [VMEM] * 7, 1 << 26, 1 << 22
    )(got, keys, values, pick, cos, sin, span)
    got = exchange(message, CHIPS)
    message = call(output_kernel, shape(RING, REQ, HD), [VMEM] * 4, 1 << 25, 1 << 22)(
        got.reshape(POOLS * INSTS, CORES, REQ, HD), back, keep, taken
    )
    got = exchange(message, RINGS)
    return call(sum_kernel, shape(1, REQ, HD), [VMEM], 1 << 17, 1 << 18)(got)


def solution(mesh):
    finer = Mesh(mesh.devices.reshape(SIZES), AXES)
    in_specs = (
        P("inst", None, ("pool",) + TP),
        P(("pool",) + TP),
        P(None, TP),
        P(("pool",) + TP, None),
        P(("pool",) + TP, None),
        P(TP, None),
        P("pool", "inst", None, None, None),
        P("pool", "inst", None, None, None),
        P(),
        P(),
        P(),
        P(),
    )
    out_specs = P("inst", None, ("pool",) + TP)
    return jax.shard_map(shards, mesh=finer, in_specs=in_specs, out_specs=out_specs, check_vma=False)
```

```python
import functools

import jax
import jax.numpy as jnp
from jax import lax
from jax.experimental import pallas as pl
from jax.experimental.pallas import tpu as pltpu
from jax.sharding import Mesh
from jax.sharding import PartitionSpec as P

HD = 128
HEADS = 4
REQ = 32
POOLS, INSTS, ZS, YS, CORES = 2, 4, 8, 2, 2
RING = ZS * POOLS
EXTRA = 8
epsilon = 1e-05
rope_base = 500000.0
AXES = ("pool", "inst", "z", "yh", "core")
SIZES = (POOLS, INSTS, ZS, YS, CORES)
TP = ("z", "yh", "core")
BF = jnp.bfloat16
F32 = jnp.float32
I32 = jnp.int32
VMEM = pl.BlockSpec(memory_space=pltpu.VMEM)
HBM = pl.BlockSpec(memory_space=pltpu.HBM)


def device_number(p, i, z, y, c):
    return (((p * INSTS + i) * ZS + z) * YS + y) * CORES + c


PLACES = [((z + 5) % ZS, 1 - y) for z in range(ZS) for y in range(YS)]
RINGS = [
    [device_number(y ^ s, i, z, y, c) for z, y in PLACES]
    for s in range(2)
    for i in range(INSTS)
    for c in range(CORES)
]


FIRST = 2
HEADS_ALIKE = [(z, y, c) for z in range(ZS) for y in range(YS) for c in range(CORES)]
TURNS = [(a, (i + FIRST) % INSTS) for a in range(POOLS) for i in range(INSTS)]
HOSTS = [[device_number(1 ^ a ^ y, i, z, y, c) for a, i in TURNS] for z, y, c in HEADS_ALIKE]
CHIPS = [
    [device_number(1 ^ a ^ y, i, z, y, c) for a, i in TURNS for c in range(CORES)]
    for z in range(ZS)
    for y in range(YS)
]


def turn(inst):
    return (inst + (INSTS - FIRST)) % INSTS


def exchange(x, groups):
    return lax.all_to_all(x, AXES, 0, 0, axis_index_groups=groups, tiled=True)


def swap_core(x):
    return lax.ppermute(x, "core", [(0, 1), (1, 0)])


def iota(shape, axis):
    return lax.broadcasted_iota(I32, shape, axis)


def dot(a, b):
    return jnp.dot(a, b, preferred_element_type=F32)


def split(x):
    high = x.astype(BF)
    return high, (x - high.astype(F32)).astype(BF)


def start_copies(pairs, sems):
    copies = [pltpu.make_async_copy(a, b, sems.at[n]) for n, (a, b) in enumerate(pairs)]
    for copy in copies:
        copy.start()
    return copies


def head_lanes(z):
    return pl.ds(pl.multiple_of((z // (ZS // HEADS)) * HD, HD), HD)


def two_rows(row):
    high = row.astype(BF).astype(F32)
    at = iota((EXTRA, HD), 0)
    return jnp.where(at == 0, high, jnp.where(at == 1, row - high, 0.0)).astype(BF)


def features_kernel(
    x_hbm, gain_hbm, wk_hbm, wv_hbm,
    scaled_out, extra_out, keep_out, give_out,
    x_ref, gain_ref, wk_ref, wv_ref, sems,
):
    pairs = ((x_hbm, x_ref), (gain_hbm, gain_ref), (wk_hbm, wk_ref), (wv_hbm, wv_ref))
    for copy in start_copies(pairs, sems):
        copy.wait()
    x = x_ref[0].astype(F32)
    scaled = (x * gain_ref[...].astype(F32)).astype(BF)
    squares = jnp.sum(x * x, axis=1, keepdims=True)
    place = iota((REQ, HD), 0) + turn(lax.axis_index("inst")) * REQ == iota((REQ, HD), 1)
    scaled_out[...] = scaled
    extra_out[...] = two_rows(jnp.sum(jnp.where(place, squares, 0.0), axis=0, keepdims=True))
    k = dot(scaled, wk_ref[...])
    v = dot(scaled, wv_ref[...])
    first = lax.axis_index("core") == 0
    keep_out[...] = jnp.where(first, k, v).astype(BF)
    give_out[...] = jnp.where(first, v, k).astype(BF)


def message_kernel(scaled_ref, extra_ref, keep_ref, taken_ref, out_ref):
    terms = (keep_ref[...].astype(F32) + taken_ref[...].astype(F32)).astype(BF)
    for m, (z, _) in enumerate(PLACES):
        n = z // (ZS // HEADS)
        out_ref[m, 0:REQ, :] = scaled_ref[...]
        out_ref[m, REQ : 2 * REQ, :] = terms[:, n * HD : (n + 1) * HD]
        out_ref[m, 2 * REQ :, :] = extra_ref[...]


def tables_kernel(
    lengths_hbm, offload_hbm, host_hbm, slot_hbm, values_hbm,
    values_out, pick_ref, back_ref, cos_ref, sin_ref, span_ref,
    lengths_ref, offload_ref, host_ref, slot_ref, sems,
):
    pool, inst = lax.axis_index("pool"), lax.axis_index("inst")
    pairs = [(lengths_hbm, lengths_ref), (offload_hbm, offload_ref), (host_hbm, host_ref), (slot_hbm, slot_ref)]
    small = len(pairs)
    pairs.append((values_hbm.at[0, 0, :, :, head_lanes(lax.axis_index("z"))], values_out))
    copies = start_copies(pairs, sems)
    for copy in copies[:small]:
        copy.wait()
    yh = lax.axis_index("yh")
    home = (1 - yh) * (INSTS * REQ) + turn(iota((INSTS, REQ), 0)) * REQ + iota((INSTS, REQ), 1)
    away = yh * (INSTS * REQ) + turn(host_ref[...]) * REQ + slot_ref[...]
    seat = jnp.where(offload_ref[...] == 1, away, home)
    spans = lengths_ref[...].astype(F32)
    here = iota((REQ, REQ), 0) + ((1 ^ pool ^ yh) * INSTS + turn(inst)) * REQ
    square = iota((REQ, REQ), 0) == iota((REQ, REQ), 1)
    pick = jnp.zeros((REQ, POOLS * INSTS * REQ), F32)
    span = jnp.zeros((REQ, 1), F32)
    column = jnp.zeros((REQ, 1), F32)
    for i in range(INSTS):
        sits = seat[i : i + 1, :] == here
        wide = iota((REQ, POOLS * INSTS * REQ), 1) % (INSTS * REQ)
        place = (wide == iota(wide.shape, 0) + turn(i) * REQ).astype(F32).astype(BF)
        pick += dot(sits.astype(F32).astype(BF), place)
        span += jnp.sum(jnp.where(sits, spans[i : i + 1, :], 0.0), axis=1, keepdims=True)
        turned = jnp.sum(jnp.where(square, seat[i : i + 1, :].astype(F32), 0.0), axis=1, keepdims=True)
        column += jnp.where(inst == i, turned, 0.0)
    pick_ref[...] = pick.astype(BF)
    seats = iota((REQ, POOLS * INSTS * REQ), 1).astype(F32)
    back_ref[...] = (column == seats).astype(F32).astype(BF)
    half = HD // 2
    lanes = iota((REQ, HD), 1)
    frequency = jnp.exp((lanes % half).astype(F32) * (-2.0 / HD * 13.122363377404328))
    angles = span * frequency
    cos_ref[...] = jnp.cos(angles)
    sin_ref[...] = jnp.where(lanes < half, -jnp.sin(angles), jnp.sin(angles))
    span_ref[...] = jnp.broadcast_to(span, (REQ, HD))
    for copy in copies[small:]:
        copy.wait()


def query_kernel(own_ref, other_ref, wq_ref, out_ref):
    core = lax.axis_index("core")
    side = lax.axis_index("pool") ^ lax.axis_index("yh")
    q = jnp.zeros((REQ, HD), F32)
    own = jnp.zeros((REQ, HD), F32)
    other = jnp.zeros((REQ, HD), F32)
    extra = jnp.zeros((EXTRA, HD), F32)
    for m, (z, y) in enumerate(PLACES):
        weight = jnp.concatenate([wq_ref[y ^ side, z, y, c] for c in (core, 1 - core)], axis=0)
        features = jnp.concatenate([own_ref[m, 0:REQ, :], other_ref[m, 0:REQ, :]], axis=1)
        q += dot(features, weight)
        own += own_ref[m, REQ : 2 * REQ, :].astype(F32)
        other += other_ref[m, REQ : 2 * REQ, :].astype(F32)
        extra += own_ref[m, 2 * REQ :, :].astype(F32) + other_ref[m, 2 * REQ :, :].astype(F32)
    first = core == 0
    k, v = jnp.where(first, own, other), jnp.where(first, other, own)
    rest = two_rows(extra[0:1] + extra[1:2])
    for m in range(POOLS * INSTS):
        for n, part in enumerate((q, k, v)):
            out_ref[m, n * REQ : (n + 1) * REQ, :] = part.astype(BF)
        out_ref[m, 3 * REQ :, :] = rest


def attend_kernel(got_ref, keys_ref, values_ref, pick_ref, cos_ref, sin_ref, span_ref, out_ref, *, width):
    pick = pick_ref[...]
    q, k, v = (dot(pick, got_ref[:, n * REQ : (n + 1) * REQ, :].reshape(pick.shape[1], HD)) for n in range(3))
    rest = jnp.zeros((EXTRA, HD), F32)
    for m in range(POOLS * INSTS):
        rest += got_ref[m, 3 * REQ :, :].astype(F32)
    squares = jnp.sum(pick[:, :HD].astype(F32) * (rest[0:1] + rest[1:2]), axis=1, keepdims=True)
    root = jnp.sqrt(squares / width + epsilon)

    def rotate(t):
        return t * cos_ref[...] + pltpu.roll(t, HD // 2, 1) * sin_ref[...]

    q = rotate(q / root).astype(BF)
    k = rotate(k / root).astype(BF)
    v = (v / root).astype(BF)
    lanes = head_lanes(lax.axis_index("z"))
    keys = keys_ref[0, 0, :, :, lanes].reshape(REQ * HD, HD)
    values = values_ref[...].reshape(REQ * HD, HD)
    every = lax.dot_general(q, keys, (((1,), (1,)), ((), ())), preferred_element_type=F32)
    request = iota((8, HD), 0)
    rows = []
    for group in range(REQ // 8):
        block = jnp.zeros((8, HD), F32)
        for n in range(8):
            r = group * 8 + n
            block = jnp.where(request == n, every[group * 8 : group * 8 + 8, r * HD : (r + 1) * HD], block)
        rows.append(block)
    factor = HD ** (-0.5)
    scores = jnp.concatenate(rows, axis=0) * factor
    own_score = jnp.sum(q.astype(F32) * k.astype(F32), axis=1, keepdims=True) * factor
    visible = iota((REQ, HD), 1).astype(F32) < span_ref[...]
    scores = jnp.where(visible, scores, -jnp.inf)
    peak = jnp.maximum(jnp.max(scores, axis=1, keepdims=True), own_score)
    exps = jnp.exp(scores - peak)
    own_exp = jnp.exp(own_score - peak)
    total = jnp.sum(exps, axis=1, keepdims=True) + own_exp
    weights = exps / total
    own_weight = (own_exp / total).astype(BF).astype(F32)
    request = iota((REQ, HD), 0)
    spread = jnp.concatenate([jnp.where(request == r, weights, 0.0).astype(BF) for r in range(REQ)], axis=1)
    mixed = (dot(spread, values) + own_weight * v.astype(F32)).astype(BF)
    for m in range(POOLS * INSTS * CORES):
        out_ref[m] = mixed


def output_kernel(got_ref, back_ref, own_ref, other_ref, out_ref):
    core = lax.axis_index("core")
    back = back_ref[...]
    seats = POOLS * INSTS * REQ
    mine = dot(back, got_ref[:, core].reshape(seats, HD)).astype(BF)
    buddy = dot(back, got_ref[:, 1 - core].reshape(seats, HD)).astype(BF)
    side = lax.axis_index("pool") ^ lax.axis_index("yh")
    parts = []
    for z, y in PLACES:
        block = (((y ^ side) * ZS + z) * YS + y) * CORES + core
        lanes = pl.ds(pl.multiple_of(block * HD, HD), HD)
        parts.append((dot(mine, own_ref[:, lanes]) + dot(buddy, other_ref[:, lanes])).astype(BF))
    for m, part in enumerate(parts):
        out_ref[m] = part


def sum_kernel(got_ref, out_ref):
    total = got_ref[0].astype(F32)
    for m in range(1, RING):
        total += got_ref[m].astype(F32)
    out_ref[0] = total.astype(BF)


def in_hbm(*arrays):
    return [pltpu.with_memory_space_constraint(a, pltpu.HBM) for a in arrays]


def call(kernel, shapes, specs, flops, moved, scratch=(), limit=24):
    one = not isinstance(shapes, list)
    return pl.pallas_call(
        kernel,
        out_shape=shapes if one else tuple(shapes),
        in_specs=specs,
        out_specs=VMEM if one else tuple(VMEM for _ in shapes),
        scratch_shapes=list(scratch),
        cost_estimate=pl.CostEstimate(flops=flops, bytes_accessed=moved, transcendentals=0),
        compiler_params=pltpu.CompilerParams(vmem_limit_bytes=limit << 20),
    )


def shape(*dims, dtype=BF):
    return jax.ShapeDtypeStruct(dims, dtype)


def shards(
    hidden_states,
    norm_gain,
    query_weight,
    key_weight,
    value_weight,
    output_weight,
    key_cache,
    value_cache,
    lengths,
    offload,
    host_instance,
    cache_slot,
):
    width = query_weight.shape[0]
    seats = POOLS * INSTS * REQ

    scaled, extra, keep, give = call(
        features_kernel,
        [shape(REQ, HD), shape(EXTRA, HD), shape(REQ, HEADS * HD), shape(REQ, HEADS * HD)],
        [HBM] * 4,
        1 << 23,
        1 << 20,
        [
            pltpu.VMEM((1, REQ, HD), BF),
            pltpu.VMEM((1, HD), BF),
            pltpu.VMEM(key_weight.shape, BF),
            pltpu.VMEM(value_weight.shape, BF),
            pltpu.SemaphoreType.DMA((4,)),
        ],
    )(*in_hbm(hidden_states, norm_gain.reshape(1, HD), key_weight, value_weight))
    message = call(message_kernel, shape(RING, 2 * REQ + EXTRA, HD), [VMEM] * 4, 1 << 14, 1 << 19)(
        scaled, extra, keep, swap_core(give)
    )
    message, output_weight = lax.optimization_barrier((message, output_weight))
    buddy_weight = swap_core(output_weight)
    got = exchange(message, RINGS)
    got, lengths, key_cache = lax.optimization_barrier((got, lengths, key_cache))
    other = swap_core(got)
    table = pltpu.VMEM(lengths.shape, I32)
    tables = call(
        tables_kernel,
        [
            shape(REQ, HD, HD),
            shape(REQ, seats),
            shape(REQ, seats),
            shape(REQ, HD, dtype=F32),
            shape(REQ, HD, dtype=F32),
            shape(REQ, HD, dtype=F32),
        ],
        [HBM] * 5,
        1 << 22,
        1 << 22,
        [table] * 4 + [pltpu.SemaphoreType.DMA((5,))],
    )(
        *in_hbm(
            lengths,
            offload,
            host_instance,
            cache_slot,
            value_cache,
        )
    )
    other, tables, buddy_weight = lax.optimization_barrier((other, tables, buddy_weight))
    values, pick, back, cos, sin, span = tables
    message = call(query_kernel, shape(POOLS * INSTS, 3 * REQ + EXTRA, HD), [VMEM] * 3, 1 << 25, 1 << 22)(got, other, query_weight.reshape(POOLS, ZS, YS, CORES, HD, HD))
    got = exchange(message, HOSTS)
    message = call(
        functools.partial(attend_kernel, width=width), shape(POOLS * INSTS * CORES, REQ, HD), [VMEM] * 7, 1 << 26, 1 << 22
    )(got, key_cache, values, pick, cos, sin, span)
    got = exchange(message, CHIPS)
    message = call(output_kernel, shape(RING, REQ, HD), [VMEM] * 4, 1 << 25, 1 << 22)(
        got.reshape(POOLS * INSTS, CORES, REQ, HD), back, output_weight, buddy_weight
    )
    got = exchange(message, RINGS)
    return call(sum_kernel, shape(1, REQ, HD), [VMEM], 1 << 17, 1 << 18)(got)


def solution(mesh):
    finer = Mesh(mesh.devices.reshape(SIZES), AXES)
    in_specs = (
        P("inst", None, ("pool",) + TP),
        P(("pool",) + TP),
        P(None, TP),
        P(("pool",) + TP, None),
        P(("pool",) + TP, None),
        P(TP, None),
        P("pool", "inst", None, None, None),
        P("pool", "inst", None, None, None),
        P(),
        P(),
        P(),
        P(),
    )
    out_specs = P("inst", None, ("pool",) + TP)
    return jax.shard_map(shards, mesh=finer, in_specs=in_specs, out_specs=out_specs, check_vma=False)
```

```python
import functools

import jax
import jax.numpy as jnp
from jax import lax
from jax.experimental import pallas as pl
from jax.experimental.pallas import tpu as pltpu
from jax.sharding import Mesh
from jax.sharding import PartitionSpec as P

HD = 128
HEADS = 4
REQ = 32
POOLS, INSTS, ZS, YS, CORES = 2, 4, 8, 2, 2
RING = ZS * POOLS
EXTRA = 8
epsilon = 1e-05
rope_base = 500000.0
AXES = ("pool", "inst", "z", "yh", "core")
SIZES = (POOLS, INSTS, ZS, YS, CORES)
TP = ("z", "yh", "core")
BF = jnp.bfloat16
F32 = jnp.float32
I32 = jnp.int32
VMEM = pl.BlockSpec(memory_space=pltpu.VMEM)
HBM = pl.BlockSpec(memory_space=pltpu.HBM)


def device_number(p, i, z, y, c):
    return (((p * INSTS + i) * ZS + z) * YS + y) * CORES + c


PLACES = [((z + 5) % ZS, 1 - y) for z in range(ZS) for y in range(YS)]
RINGS = [
    [device_number(y ^ s, i, z, y, c) for z, y in PLACES]
    for s in range(2)
    for i in range(INSTS)
    for c in range(CORES)
]


FIRST = 2
HEADS_ALIKE = [(z, y, c) for z in range(ZS) for y in range(YS) for c in range(CORES)]
TURNS = [(a, (i + FIRST) % INSTS) for a in range(POOLS) for i in range(INSTS)]
HOSTS = [[device_number(1 ^ a ^ y, i, z, y, c) for a, i in TURNS] for z, y, c in HEADS_ALIKE]
CHIPS = [
    [device_number(1 ^ a ^ y, i, z, y, c) for a, i in TURNS for c in range(CORES)]
    for z in range(ZS)
    for y in range(YS)
]


def turn(inst):
    return (inst + (INSTS - FIRST)) % INSTS


def exchange(x, groups):
    return lax.all_to_all(x, AXES, 0, 0, axis_index_groups=groups, tiled=True)


def swap_core(x):
    return lax.ppermute(x, "core", [(0, 1), (1, 0)])


def iota(shape, axis):
    return lax.broadcasted_iota(I32, shape, axis)


def dot(a, b):
    return jnp.dot(a, b, preferred_element_type=F32)


def split(x):
    high = x.astype(BF)
    return high, (x - high.astype(F32)).astype(BF)


def start_copies(pairs, sems):
    copies = [pltpu.make_async_copy(a, b, sems.at[n]) for n, (a, b) in enumerate(pairs)]
    for copy in copies:
        copy.start()
    return copies


def head_lanes(z):
    return pl.ds(pl.multiple_of((z // (ZS // HEADS)) * HD, HD), HD)


def two_rows(row):
    high = row.astype(BF).astype(F32)
    at = iota((EXTRA, HD), 0)
    return jnp.where(at == 0, high, jnp.where(at == 1, row - high, 0.0)).astype(BF)


def features_kernel(
    x_hbm, gain_hbm, wk_hbm, wv_hbm,
    scaled_out, extra_out, keep_out, give_out,
    x_ref, gain_ref, wk_ref, wv_ref, sems,
):
    pairs = ((x_hbm, x_ref), (gain_hbm, gain_ref), (wk_hbm, wk_ref), (wv_hbm, wv_ref))
    for copy in start_copies(pairs, sems):
        copy.wait()
    x = x_ref[0].astype(F32)
    scaled = (x * gain_ref[...].astype(F32)).astype(BF)
    squares = jnp.sum(x * x, axis=1, keepdims=True)
    place = iota((REQ, HD), 0) + turn(lax.axis_index("inst")) * REQ == iota((REQ, HD), 1)
    scaled_out[...] = scaled
    extra_out[...] = two_rows(jnp.sum(jnp.where(place, squares, 0.0), axis=0, keepdims=True))
    k = dot(scaled, wk_ref[...])
    v = dot(scaled, wv_ref[...])
    first = lax.axis_index("core") == 0
    keep_out[...] = jnp.where(first, k, v).astype(BF)
    give_out[...] = jnp.where(first, v, k).astype(BF)


def message_kernel(scaled_ref, extra_ref, keep_ref, taken_ref, out_ref):
    terms = (keep_ref[...].astype(F32) + taken_ref[...].astype(F32)).astype(BF)
    for m, (z, _) in enumerate(PLACES):
        n = z // (ZS // HEADS)
        out_ref[m, 0:REQ, :] = scaled_ref[...]
        out_ref[m, REQ : 2 * REQ, :] = terms[:, n * HD : (n + 1) * HD]
        out_ref[m, 2 * REQ :, :] = extra_ref[...]


def tables_kernel(
    lengths_hbm, offload_hbm, host_hbm, slot_hbm, values_hbm,
    values_out, pick_ref, back_ref, cos_ref, sin_ref, span_ref,
    lengths_ref, offload_ref, host_ref, slot_ref, sems,
):
    pool, inst = lax.axis_index("pool"), lax.axis_index("inst")
    pairs = [(lengths_hbm, lengths_ref), (offload_hbm, offload_ref), (host_hbm, host_ref), (slot_hbm, slot_ref)]
    small = len(pairs)
    pairs.append((values_hbm.at[0, 0, :, :, head_lanes(lax.axis_index("z"))], values_out))
    copies = start_copies(pairs, sems)
    for copy in copies[:small]:
        copy.wait()
    yh = lax.axis_index("yh")
    home = (1 - yh) * (INSTS * REQ) + turn(iota((INSTS, REQ), 0)) * REQ + iota((INSTS, REQ), 1)
    away = yh * (INSTS * REQ) + turn(host_ref[...]) * REQ + slot_ref[...]
    seat = jnp.where(offload_ref[...] == 1, away, home)
    spans = lengths_ref[...].astype(F32)
    here = iota((REQ, REQ), 0) + ((1 ^ pool ^ yh) * INSTS + turn(inst)) * REQ
    square = iota((REQ, REQ), 0) == iota((REQ, REQ), 1)
    pick = jnp.zeros((REQ, POOLS * INSTS * REQ), F32)
    span = jnp.zeros((REQ, 1), F32)
    column = jnp.zeros((REQ, 1), F32)
    for i in range(INSTS):
        sits = seat[i : i + 1, :] == here
        wide = iota((REQ, POOLS * INSTS * REQ), 1) % (INSTS * REQ)
        place = (wide == iota(wide.shape, 0) + turn(i) * REQ).astype(F32).astype(BF)
        pick += dot(sits.astype(F32).astype(BF), place)
        span += jnp.sum(jnp.where(sits, spans[i : i + 1, :], 0.0), axis=1, keepdims=True)
        turned = jnp.sum(jnp.where(square, seat[i : i + 1, :].astype(F32), 0.0), axis=1, keepdims=True)
        column += jnp.where(inst == i, turned, 0.0)
    pick_ref[...] = pick.astype(BF)
    seats = iota((REQ, POOLS * INSTS * REQ), 1).astype(F32)
    back_ref[...] = (column == seats).astype(F32).astype(BF)
    half = HD // 2
    lanes = iota((REQ, HD), 1)
    frequency = jnp.exp((lanes % half).astype(F32) * (-2.0 / HD * 13.122363377404328))
    angles = span * frequency
    cos_ref[...] = jnp.cos(angles)
    sin_ref[...] = jnp.where(lanes < half, -jnp.sin(angles), jnp.sin(angles))
    span_ref[...] = jnp.broadcast_to(span, (REQ, HD))
    for copy in copies[small:]:
        copy.wait()


def query_kernel(own_ref, other_ref, wq_ref, out_ref):
    core = lax.axis_index("core")
    side = lax.axis_index("pool") ^ lax.axis_index("yh")
    q = jnp.zeros((REQ, HD), F32)
    own = jnp.zeros((REQ, HD), F32)
    other = jnp.zeros((REQ, HD), F32)
    extra = jnp.zeros((EXTRA, HD), F32)
    for m, (z, y) in enumerate(PLACES):
        weight = jnp.concatenate([wq_ref[y ^ side, z, y, c] for c in (core, 1 - core)], axis=0)
        features = jnp.concatenate([own_ref[m, 0:REQ, :], other_ref[m, 0:REQ, :]], axis=1)
        q += dot(features, weight)
        own += own_ref[m, REQ : 2 * REQ, :].astype(F32)
        other += other_ref[m, REQ : 2 * REQ, :].astype(F32)
        extra += own_ref[m, 2 * REQ :, :].astype(F32) + other_ref[m, 2 * REQ :, :].astype(F32)
    first = core == 0
    k, v = jnp.where(first, own, other), jnp.where(first, other, own)
    rest = two_rows(extra[0:1] + extra[1:2])
    for m in range(POOLS * INSTS):
        for n, part in enumerate((q, k, v)):
            out_ref[m, n * REQ : (n + 1) * REQ, :] = part.astype(BF)
        out_ref[m, 3 * REQ :, :] = rest


def attend_kernel(got_ref, keys_ref, values_ref, pick_ref, cos_ref, sin_ref, span_ref, out_ref, *, width):
    pick = pick_ref[...]
    q, k, v = (dot(pick, got_ref[:, n * REQ : (n + 1) * REQ, :].reshape(pick.shape[1], HD)) for n in range(3))
    rest = jnp.zeros((EXTRA, HD), F32)
    for m in range(POOLS * INSTS):
        rest += got_ref[m, 3 * REQ :, :].astype(F32)
    squares = jnp.sum(pick[:, :HD].astype(F32) * (rest[0:1] + rest[1:2]), axis=1, keepdims=True)
    root = jnp.sqrt(squares / width + epsilon)

    def rotate(t):
        return t * cos_ref[...] + pltpu.roll(t, HD // 2, 1) * sin_ref[...]

    q = rotate(q).astype(BF)
    k = rotate(k).astype(BF)
    v = (v / root).astype(BF)
    lanes = head_lanes(lax.axis_index("z"))
    keys = keys_ref[0, 0, :, :, lanes].reshape(REQ * HD, HD)
    values = values_ref[...].reshape(REQ * HD, HD)
    every = lax.dot_general(q, keys, (((1,), (1,)), ((), ())), preferred_element_type=F32)
    request = iota((8, HD), 0)
    rows = []
    for group in range(REQ // 8):
        block = jnp.zeros((8, HD), F32)
        for n in range(8):
            r = group * 8 + n
            block = jnp.where(request == n, every[group * 8 : group * 8 + 8, r * HD : (r + 1) * HD], block)
        rows.append(block)
    scale = HD ** (-0.5) / root
    scores = jnp.concatenate(rows, axis=0) * scale
    own_score = jnp.sum(q.astype(F32) * k.astype(F32), axis=1, keepdims=True) * (scale / root)
    visible = iota((REQ, HD), 1).astype(F32) < span_ref[...]
    scores = jnp.where(visible, scores, -jnp.inf)
    peak = jnp.maximum(jnp.max(scores, axis=1, keepdims=True), -1e30)
    exps = jnp.exp(scores - peak)
    request = iota((REQ, HD), 0)
    spread = jnp.concatenate([jnp.where(request == r, exps, 0.0).astype(BF) for r in range(REQ)], axis=1)
    mixed = dot(spread, values)
    top = jnp.maximum(peak, own_score)
    cached, own = jnp.exp(peak - top), jnp.exp(own_score - top)
    total = jnp.sum(exps, axis=1, keepdims=True) * cached + own
    mixed = (mixed * (cached / total) + (own / total) * v.astype(F32)).astype(BF)
    for m in range(POOLS * INSTS * CORES):
        out_ref[m] = mixed


def output_kernel(got_ref, back_ref, own_ref, other_ref, out_ref):
    core = lax.axis_index("core")
    back = back_ref[...]
    seats = POOLS * INSTS * REQ
    mine = dot(back, got_ref[:, core].reshape(seats, HD)).astype(BF)
    buddy = dot(back, got_ref[:, 1 - core].reshape(seats, HD)).astype(BF)
    side = lax.axis_index("pool") ^ lax.axis_index("yh")
    rows = jnp.concatenate([mine, buddy], axis=1)
    parts = []
    for m in range(0, RING, 2):
        weights = []
        for z, y in PLACES[m : m + 2]:
            block = (((y ^ side) * ZS + z) * YS + y) * CORES + core
            lanes = pl.ds(pl.multiple_of(block * HD, HD), HD)
            weights.append(jnp.concatenate([own_ref[:, lanes], other_ref[:, lanes]], axis=0))
        two = dot(rows, jnp.concatenate(weights, axis=1)).astype(BF)
        parts += [two[:, :HD], two[:, HD:]]
    for m, part in enumerate(parts):
        out_ref[m] = part


def sum_kernel(got_ref, out_ref):
    total = got_ref[0].astype(F32)
    for m in range(1, RING):
        total += got_ref[m].astype(F32)
    out_ref[0] = total.astype(BF)


def in_hbm(*arrays):
    return [pltpu.with_memory_space_constraint(a, pltpu.HBM) for a in arrays]


def call(kernel, shapes, specs, flops, moved, scratch=(), limit=24):
    one = not isinstance(shapes, list)
    return pl.pallas_call(
        kernel,
        out_shape=shapes if one else tuple(shapes),
        in_specs=specs,
        out_specs=VMEM if one else tuple(VMEM for _ in shapes),
        scratch_shapes=list(scratch),
        cost_estimate=pl.CostEstimate(flops=flops, bytes_accessed=moved, transcendentals=0),
        compiler_params=pltpu.CompilerParams(vmem_limit_bytes=limit << 20),
    )


def shape(*dims, dtype=BF):
    return jax.ShapeDtypeStruct(dims, dtype)


def shards(
    hidden_states,
    norm_gain,
    query_weight,
    key_weight,
    value_weight,
    output_weight,
    key_cache,
    value_cache,
    lengths,
    offload,
    host_instance,
    cache_slot,
):
    width = query_weight.shape[0]
    seats = POOLS * INSTS * REQ

    scaled, extra, keep, give = call(
        features_kernel,
        [shape(REQ, HD), shape(EXTRA, HD), shape(REQ, HEADS * HD), shape(REQ, HEADS * HD)],
        [HBM] * 4,
        1 << 23,
        1 << 20,
        [
            pltpu.VMEM((1, REQ, HD), BF),
            pltpu.VMEM((1, HD), BF),
            pltpu.VMEM(key_weight.shape, BF),
            pltpu.VMEM(value_weight.shape, BF),
            pltpu.SemaphoreType.DMA((4,)),
        ],
    )(*in_hbm(hidden_states, norm_gain.reshape(1, HD), key_weight, value_weight))
    message = call(message_kernel, shape(RING, 2 * REQ + EXTRA, HD), [VMEM] * 4, 1 << 14, 1 << 19)(
        scaled, extra, keep, swap_core(give)
    )
    message, output_weight = lax.optimization_barrier((message, output_weight))
    buddy_weight = swap_core(output_weight)
    got = exchange(message, RINGS)
    got, lengths, key_cache = lax.optimization_barrier((got, lengths, key_cache))
    other = swap_core(got)
    table = pltpu.VMEM(lengths.shape, I32)
    tables = call(
        tables_kernel,
        [
            shape(REQ, HD, HD),
            shape(REQ, seats),
            shape(REQ, seats),
            shape(REQ, HD, dtype=F32),
            shape(REQ, HD, dtype=F32),
            shape(REQ, HD, dtype=F32),
        ],
        [HBM] * 5,
        1 << 22,
        1 << 22,
        [table] * 4 + [pltpu.SemaphoreType.DMA((5,))],
    )(
        *in_hbm(
            lengths,
            offload,
            host_instance,
            cache_slot,
            value_cache,
        )
    )
    other, tables, buddy_weight = lax.optimization_barrier((other, tables, buddy_weight))
    values, pick, back, cos, sin, span = tables
    message = call(query_kernel, shape(POOLS * INSTS, 3 * REQ + EXTRA, HD), [VMEM] * 3, 1 << 25, 1 << 22)(got, other, query_weight.reshape(POOLS, ZS, YS, CORES, HD, HD))
    got = exchange(message, HOSTS)
    message = call(
        functools.partial(attend_kernel, width=width), shape(POOLS * INSTS * CORES, REQ, HD), [VMEM] * 7, 1 << 26, 1 << 22
    )(got, key_cache, values, pick, cos, sin, span)
    got = exchange(message, CHIPS)
    message = call(output_kernel, shape(RING, REQ, HD), [VMEM] * 4, 1 << 25, 1 << 22)(
        got.reshape(POOLS * INSTS, CORES, REQ, HD), back, output_weight, buddy_weight
    )
    got = exchange(message, RINGS)
    return call(sum_kernel, shape(1, REQ, HD), [VMEM], 1 << 17, 1 << 18)(got)


def solution(mesh):
    finer = Mesh(mesh.devices.reshape(SIZES), AXES)
    in_specs = (
        P("inst", None, ("pool",) + TP),
        P(("pool",) + TP),
        P(None, TP),
        P(("pool",) + TP, None),
        P(("pool",) + TP, None),
        P(TP, None),
        P("pool", "inst", None, None, None),
        P("pool", "inst", None, None, None),
        P(),
        P(),
        P(),
        P(),
    )
    out_specs = P("inst", None, ("pool",) + TP)
    return jax.shard_map(shards, mesh=finer, in_specs=in_specs, out_specs=out_specs, check_vma=False)
```

```python
import functools

import jax
import jax.numpy as jnp
from jax import lax
from jax.experimental import pallas as pl
from jax.experimental.pallas import tpu as pltpu
from jax.sharding import Mesh
from jax.sharding import PartitionSpec as P

HD = 128
HEADS = 4
REQ = 32
POOLS, INSTS, ZS, YS, CORES = 2, 4, 8, 2, 2
RING = ZS * POOLS
EXTRA = 16
epsilon = 1e-05
rope_base = 500000.0
AXES = ("pool", "inst", "z", "yh", "core")
SIZES = (POOLS, INSTS, ZS, YS, CORES)
TP = ("z", "yh", "core")
BF = jnp.bfloat16
F32 = jnp.float32
I32 = jnp.int32
VMEM = pl.BlockSpec(memory_space=pltpu.VMEM)
HBM = pl.BlockSpec(memory_space=pltpu.HBM)


def device_number(p, i, z, y, c):
    return (((p * INSTS + i) * ZS + z) * YS + y) * CORES + c


PLACES = [((z + 5) % ZS, 1 - y) for z in range(ZS) for y in range(YS)]
RINGS = [
    [device_number(y ^ s, i, z, y, c) for z, y in PLACES]
    for s in range(2)
    for i in range(INSTS)
    for c in range(CORES)
]


FIRST = 2
HEADS_ALIKE = [(z, y, c) for z in range(ZS) for y in range(YS) for c in range(CORES)]
TURNS = [(a, (i + FIRST) % INSTS) for a in range(POOLS) for i in range(INSTS)]
HOSTS = [[device_number(1 ^ a ^ y, i, z, y, c) for a, i in TURNS] for z, y, c in HEADS_ALIKE]
CHIPS = [
    [device_number(1 ^ a ^ y, i, z, y, c) for a, i in TURNS for c in range(CORES)]
    for z in range(ZS)
    for y in range(YS)
]


def turn(inst):
    return (inst + (INSTS - FIRST)) % INSTS


def exchange(x, groups):
    return lax.all_to_all(x, AXES, 0, 0, axis_index_groups=groups, tiled=True)


def swap_core(x):
    return lax.ppermute(x, "core", [(0, 1), (1, 0)])


def iota(shape, axis):
    return lax.broadcasted_iota(I32, shape, axis)


def dot(a, b):
    return jnp.dot(a, b, preferred_element_type=F32)


def split(x):
    high = x.astype(BF)
    return high, (x - high.astype(F32)).astype(BF)


def start_copies(pairs, sems):
    copies = [pltpu.make_async_copy(a, b, sems.at[n]) for n, (a, b) in enumerate(pairs)]
    for copy in copies:
        copy.start()
    return copies


def head_lanes(z):
    return pl.ds(pl.multiple_of((z // (ZS // HEADS)) * HD, HD), HD)


def two_rows(row):
    high = row.astype(BF).astype(F32)
    at = iota((EXTRA, HD), 0)
    return jnp.where(at == 0, high, jnp.where(at == 1, row - high, 0.0)).astype(BF)


def features_kernel(
    x_hbm, gain_hbm, wk_hbm, wv_hbm,
    scaled_out, extra_out, keep_out, give_out,
    x_ref, gain_ref, wk_ref, wv_ref, sems,
):
    pairs = ((x_hbm, x_ref), (gain_hbm, gain_ref), (wk_hbm, wk_ref), (wv_hbm, wv_ref))
    for copy in start_copies(pairs, sems):
        copy.wait()
    x = x_ref[0].astype(F32)
    scaled = (x * gain_ref[...].astype(F32)).astype(BF)
    squares = jnp.sum(x * x, axis=1, keepdims=True)
    place = iota((REQ, HD), 0) + turn(lax.axis_index("inst")) * REQ == iota((REQ, HD), 1)
    scaled_out[...] = scaled
    extra_out[...] = two_rows(jnp.sum(jnp.where(place, squares, 0.0), axis=0, keepdims=True))
    k = dot(scaled, wk_ref[...])
    v = dot(scaled, wv_ref[...])
    first = lax.axis_index("core") == 0
    keep_out[...] = jnp.where(first, k, v).astype(BF)
    give_out[...] = jnp.where(first, v, k).astype(BF)


def message_kernel(scaled_ref, extra_ref, keep_ref, taken_ref, out_ref):
    terms = (keep_ref[...].astype(F32) + taken_ref[...].astype(F32)).astype(BF)
    for m, (z, _) in enumerate(PLACES):
        n = z // (ZS // HEADS)
        out_ref[m, 0:REQ, :] = scaled_ref[...]
        out_ref[m, REQ : 2 * REQ, :] = terms[:, n * HD : (n + 1) * HD]
        out_ref[m, 2 * REQ :, :] = extra_ref[...]


def tables_kernel(
    lengths_hbm, offload_hbm, host_hbm, slot_hbm, values_hbm,
    values_out, pick_ref, back_ref, cos_ref, sin_ref, span_ref,
    lengths_ref, offload_ref, host_ref, slot_ref, sems,
):
    pool, inst = lax.axis_index("pool"), lax.axis_index("inst")
    pairs = [(lengths_hbm, lengths_ref), (offload_hbm, offload_ref), (host_hbm, host_ref), (slot_hbm, slot_ref)]
    small = len(pairs)
    pairs.append((values_hbm.at[0, 0, :, :, head_lanes(lax.axis_index("z"))], values_out))
    copies = start_copies(pairs, sems)
    for copy in copies[:small]:
        copy.wait()
    yh = lax.axis_index("yh")
    home = (1 - yh) * (INSTS * REQ) + turn(iota((INSTS, REQ), 0)) * REQ + iota((INSTS, REQ), 1)
    away = yh * (INSTS * REQ) + turn(host_ref[...]) * REQ + slot_ref[...]
    seat = jnp.where(offload_ref[...] == 1, away, home)
    spans = lengths_ref[...].astype(F32)
    here = iota((REQ, REQ), 0) + ((1 ^ pool ^ yh) * INSTS + turn(inst)) * REQ
    square = iota((REQ, REQ), 0) == iota((REQ, REQ), 1)
    pick = jnp.zeros((REQ, POOLS * INSTS * REQ), F32)
    span = jnp.zeros((REQ, 1), F32)
    column = jnp.zeros((REQ, 1), F32)
    for i in range(INSTS):
        sits = seat[i : i + 1, :] == here
        wide = iota((REQ, POOLS * INSTS * REQ), 1) % (INSTS * REQ)
        place = (wide == iota(wide.shape, 0) + turn(i) * REQ).astype(F32).astype(BF)
        pick += dot(sits.astype(F32).astype(BF), place)
        span += jnp.sum(jnp.where(sits, spans[i : i + 1, :], 0.0), axis=1, keepdims=True)
        turned = jnp.sum(jnp.where(square, seat[i : i + 1, :].astype(F32), 0.0), axis=1, keepdims=True)
        column += jnp.where(inst == i, turned, 0.0)
    pick_ref[...] = pick.astype(BF)
    seats = iota((REQ, POOLS * INSTS * REQ), 1).astype(F32)
    back_ref[...] = (column == seats).astype(F32).astype(BF)
    half = HD // 2
    lanes = iota((REQ, HD), 1)
    frequency = jnp.exp((lanes % half).astype(F32) * (-2.0 / HD * 13.122363377404328))
    angles = span * frequency
    cos_ref[...] = jnp.cos(angles)
    sin_ref[...] = jnp.where(lanes < half, -jnp.sin(angles), jnp.sin(angles))
    span_ref[...] = jnp.broadcast_to(span, (REQ, HD))
    for copy in copies[small:]:
        copy.wait()


def query_kernel(own_ref, other_ref, wq_ref, out_ref):
    core = lax.axis_index("core")
    side = lax.axis_index("pool") ^ lax.axis_index("yh")
    q = jnp.zeros((REQ, HD), F32)
    own = jnp.zeros((REQ, HD), F32)
    other = jnp.zeros((REQ, HD), F32)
    extra = jnp.zeros((EXTRA, HD), F32)
    for m, (z, y) in enumerate(PLACES):
        weight = jnp.concatenate([wq_ref[y ^ side, z, y, c] for c in (core, 1 - core)], axis=0)
        features = jnp.concatenate([own_ref[m, 0:REQ, :], other_ref[m, 0:REQ, :]], axis=1)
        q += dot(features, weight)
        own += own_ref[m, REQ : 2 * REQ, :].astype(F32)
        other += other_ref[m, REQ : 2 * REQ, :].astype(F32)
        extra += own_ref[m, 2 * REQ :, :].astype(F32) + other_ref[m, 2 * REQ :, :].astype(F32)
    first = core == 0
    k, v = jnp.where(first, own, other), jnp.where(first, other, own)
    rest = two_rows(extra[0:1] + extra[1:2])
    for m in range(POOLS * INSTS):
        for n, part in enumerate((q, k, v)):
            out_ref[m, n * REQ : (n + 1) * REQ, :] = part.astype(BF)
        out_ref[m, 3 * REQ :, :] = rest


def attend_kernel(got_ref, keys_ref, values_ref, pick_ref, cos_ref, sin_ref, span_ref, out_ref, *, width):
    pick = pick_ref[...]
    q, k, v = (dot(pick, got_ref[:, n * REQ : (n + 1) * REQ, :].reshape(pick.shape[1], HD)) for n in range(3))
    rest = jnp.zeros((EXTRA, HD), F32)
    for m in range(POOLS * INSTS):
        rest += got_ref[m, 3 * REQ :, :].astype(F32)
    squares = jnp.sum(pick[:, :HD].astype(F32) * (rest[0:1] + rest[1:2]), axis=1, keepdims=True)
    root = jnp.sqrt(squares / width + epsilon)

    def rotate(t):
        return t * cos_ref[...] + pltpu.roll(t, HD // 2, 1) * sin_ref[...]

    q = rotate(q).astype(BF)
    k = rotate(k).astype(BF)
    v = (v / root).astype(BF)
    lanes = head_lanes(lax.axis_index("z"))
    keys = keys_ref[0, 0, :, :, lanes].reshape(REQ * HD, HD)
    values = values_ref[...].reshape(REQ * HD, HD)
    every = lax.dot_general(q, keys, (((1,), (1,)), ((), ())), preferred_element_type=F32)
    request = iota((8, HD), 0)
    rows = []
    for group in range(REQ // 8):
        block = jnp.zeros((8, HD), F32)
        for n in range(8):
            r = group * 8 + n
            block = jnp.where(request == n, every[group * 8 : group * 8 + 8, r * HD : (r + 1) * HD], block)
        rows.append(block)
    scale = HD ** (-0.5) / root
    scores = jnp.concatenate(rows, axis=0) * scale
    own_score = jnp.sum(q.astype(F32) * k.astype(F32), axis=1, keepdims=True) * (scale / root)
    visible = iota((REQ, HD), 1).astype(F32) < span_ref[...]
    scores = jnp.where(visible, scores, -jnp.inf)
    peak = jnp.maximum(jnp.max(scores, axis=1, keepdims=True), -1e30)
    exps = jnp.exp(scores - peak)
    request = iota((REQ, HD), 0)
    spread = jnp.concatenate([jnp.where(request == r, exps, 0.0).astype(BF) for r in range(REQ)], axis=1)
    mixed = dot(spread, values)
    top = jnp.maximum(peak, own_score)
    cached, own = jnp.exp(peak - top), jnp.exp(own_score - top)
    total = jnp.sum(exps, axis=1, keepdims=True) * cached + own
    mixed = (mixed * (cached / total) + (own / total) * v.astype(F32)).astype(BF)
    for m in range(POOLS * INSTS * CORES):
        out_ref[m] = mixed


def output_kernel(got_ref, back_ref, own_ref, other_ref, out_ref):
    core = lax.axis_index("core")
    back = back_ref[...]
    seats = POOLS * INSTS * REQ
    mine = dot(back, got_ref[:, core].reshape(seats, HD)).astype(BF)
    buddy = dot(back, got_ref[:, 1 - core].reshape(seats, HD)).astype(BF)
    side = lax.axis_index("pool") ^ lax.axis_index("yh")
    rows = jnp.concatenate([mine, buddy], axis=1)
    parts = []
    for m in range(0, RING, 2):
        weights = []
        for z, y in PLACES[m : m + 2]:
            block = (((y ^ side) * ZS + z) * YS + y) * CORES + core
            lanes = pl.ds(pl.multiple_of(block * HD, HD), HD)
            weights.append(jnp.concatenate([own_ref[:, lanes], other_ref[:, lanes]], axis=0))
        two = dot(rows, jnp.concatenate(weights, axis=1)).astype(BF)
        parts += [two[:, :HD], two[:, HD:]]
    for m, part in enumerate(parts):
        out_ref[m] = part


def sum_kernel(got_ref, out_ref):
    total = got_ref[0].astype(F32)
    for m in range(1, RING):
        total += got_ref[m].astype(F32)
    out_ref[0] = total.astype(BF)


def in_hbm(*arrays):
    return [pltpu.with_memory_space_constraint(a, pltpu.HBM) for a in arrays]


def call(kernel, shapes, specs, flops, moved, scratch=(), limit=24):
    one = not isinstance(shapes, list)
    return pl.pallas_call(
        kernel,
        out_shape=shapes if one else tuple(shapes),
        in_specs=specs,
        out_specs=VMEM if one else tuple(VMEM for _ in shapes),
        scratch_shapes=list(scratch),
        cost_estimate=pl.CostEstimate(flops=flops, bytes_accessed=moved, transcendentals=0),
        compiler_params=pltpu.CompilerParams(vmem_limit_bytes=limit << 20),
    )


def shape(*dims, dtype=BF):
    return jax.ShapeDtypeStruct(dims, dtype)


def shards(
    hidden_states,
    norm_gain,
    query_weight,
    key_weight,
    value_weight,
    output_weight,
    key_cache,
    value_cache,
    lengths,
    offload,
    host_instance,
    cache_slot,
):
    width = query_weight.shape[0]
    seats = POOLS * INSTS * REQ

    scaled, extra, keep, give = call(
        features_kernel,
        [shape(REQ, HD), shape(EXTRA, HD), shape(REQ, HEADS * HD), shape(REQ, HEADS * HD)],
        [HBM] * 4,
        1 << 23,
        1 << 20,
        [
            pltpu.VMEM((1, REQ, HD), BF),
            pltpu.VMEM((1, HD), BF),
            pltpu.VMEM(key_weight.shape, BF),
            pltpu.VMEM(value_weight.shape, BF),
            pltpu.SemaphoreType.DMA((4,)),
        ],
    )(*in_hbm(hidden_states, norm_gain.reshape(1, HD), key_weight, value_weight))
    message = call(message_kernel, shape(RING, 2 * REQ + EXTRA, HD), [VMEM] * 4, 1 << 14, 1 << 19)(
        scaled, extra, keep, swap_core(give)
    )
    message, output_weight = lax.optimization_barrier((message, output_weight))
    buddy_weight = swap_core(output_weight)
    got = exchange(message, RINGS)
    got, lengths, key_cache = lax.optimization_barrier((got, lengths, key_cache))
    other = swap_core(got)
    table = pltpu.VMEM(lengths.shape, I32)
    tables = call(
        tables_kernel,
        [
            shape(REQ, HD, HD),
            shape(REQ, seats),
            shape(REQ, seats),
            shape(REQ, HD, dtype=F32),
            shape(REQ, HD, dtype=F32),
            shape(REQ, HD, dtype=F32),
        ],
        [HBM] * 5,
        1 << 22,
        1 << 22,
        [table] * 4 + [pltpu.SemaphoreType.DMA((5,))],
    )(
        *in_hbm(
            lengths,
            offload,
            host_instance,
            cache_slot,
            value_cache,
        )
    )
    other, tables, buddy_weight = lax.optimization_barrier((other, tables, buddy_weight))
    values, pick, back, cos, sin, span = tables
    message = call(query_kernel, shape(POOLS * INSTS, 3 * REQ + EXTRA, HD), [VMEM] * 3, 1 << 25, 1 << 22)(got, other, query_weight.reshape(POOLS, ZS, YS, CORES, HD, HD))
    got = exchange(message, HOSTS)
    message = call(
        functools.partial(attend_kernel, width=width), shape(POOLS * INSTS * CORES, REQ, HD), [VMEM] * 7, 1 << 26, 1 << 22
    )(got, key_cache, values, pick, cos, sin, span)
    got = exchange(message, CHIPS)
    message = call(output_kernel, shape(RING, REQ, HD), [VMEM] * 4, 1 << 25, 1 << 22)(
        got.reshape(POOLS * INSTS, CORES, REQ, HD), back, output_weight, buddy_weight
    )
    got = exchange(message, RINGS)
    return call(sum_kernel, shape(1, REQ, HD), [VMEM], 1 << 17, 1 << 18)(got)


def solution(mesh):
    finer = Mesh(mesh.devices.reshape(SIZES), AXES)
    in_specs = (
        P("inst", None, ("pool",) + TP),
        P(("pool",) + TP),
        P(None, TP),
        P(("pool",) + TP, None),
        P(("pool",) + TP, None),
        P(TP, None),
        P("pool", "inst", None, None, None),
        P("pool", "inst", None, None, None),
        P(),
        P(),
        P(),
        P(),
    )
    out_specs = P("inst", None, ("pool",) + TP)
    return jax.shard_map(shards, mesh=finer, in_specs=in_specs, out_specs=out_specs, check_vma=False)
```

```python
import functools

import jax
import jax.numpy as jnp
from jax import lax
from jax.experimental import pallas as pl
from jax.experimental.pallas import tpu as pltpu
from jax.sharding import Mesh
from jax.sharding import PartitionSpec as P

HD = 128
HEADS = 4
REQ = 32
POOLS, INSTS, ZS, YS, CORES = 2, 4, 8, 2, 2
RING = ZS * POOLS
EXTRA = 8
epsilon = 1e-05
rope_base = 500000.0
AXES = ("pool", "inst", "z", "yh", "core")
SIZES = (POOLS, INSTS, ZS, YS, CORES)
TP = ("z", "yh", "core")
BF = jnp.bfloat16
F32 = jnp.float32
I32 = jnp.int32
VMEM = pl.BlockSpec(memory_space=pltpu.VMEM)
HBM = pl.BlockSpec(memory_space=pltpu.HBM)


def device_number(p, i, z, y, c):
    return (((p * INSTS + i) * ZS + z) * YS + y) * CORES + c


PLACES = [((z + 5) % ZS, 1 - y) for z in range(ZS) for y in range(YS)]
RINGS = [
    [device_number(y ^ s, i, z, y, c) for z, y in PLACES]
    for s in range(2)
    for i in range(INSTS)
    for c in range(CORES)
]


FIRST = 2
HEADS_ALIKE = [(z, y, c) for z in range(ZS) for y in range(YS) for c in range(CORES)]
TURNS = [(a, (i + FIRST) % INSTS) for a in range(POOLS) for i in range(INSTS)]
HOSTS = [[device_number(a ^ y, i, z, y, c) for a, i in TURNS] for z, y, c in HEADS_ALIKE]
CHIPS = [
    [device_number(1 ^ a ^ y, i, z, y, c) for a, i in TURNS for c in range(CORES)]
    for z in range(ZS)
    for y in range(YS)
]


def turn(inst):
    return (inst + (INSTS - FIRST)) % INSTS


def exchange(x, groups):
    return lax.all_to_all(x, AXES, 0, 0, axis_index_groups=groups, tiled=True)


def swap_core(x):
    return lax.ppermute(x, "core", [(0, 1), (1, 0)])


def iota(shape, axis):
    return lax.broadcasted_iota(I32, shape, axis)


def dot(a, b):
    return jnp.dot(a, b, preferred_element_type=F32)


def split(x):
    high = x.astype(BF)
    return high, (x - high.astype(F32)).astype(BF)


def start_copies(pairs, sems):
    copies = [pltpu.make_async_copy(a, b, sems.at[n]) for n, (a, b) in enumerate(pairs)]
    for copy in copies:
        copy.start()
    return copies


def head_lanes(z):
    return pl.ds(pl.multiple_of((z // (ZS // HEADS)) * HD, HD), HD)


def two_rows(row):
    high = row.astype(BF).astype(F32)
    at = iota((EXTRA, HD), 0)
    return jnp.where(at == 0, high, jnp.where(at == 1, row - high, 0.0)).astype(BF)


def features_kernel(
    x_hbm, gain_hbm, wk_hbm, wv_hbm,
    scaled_out, extra_out, keep_out, give_out,
    x_ref, gain_ref, wk_ref, wv_ref, sems,
):
    pairs = ((x_hbm, x_ref), (gain_hbm, gain_ref), (wk_hbm, wk_ref), (wv_hbm, wv_ref))
    for copy in start_copies(pairs, sems):
        copy.wait()
    x = x_ref[0].astype(F32)
    scaled = (x * gain_ref[...].astype(F32)).astype(BF)
    squares = jnp.sum(x * x, axis=1, keepdims=True)
    place = iota((REQ, HD), 0) + turn(lax.axis_index("inst")) * REQ == iota((REQ, HD), 1)
    scaled_out[...] = scaled
    extra_out[...] = two_rows(jnp.sum(jnp.where(place, squares, 0.0), axis=0, keepdims=True))
    k = dot(scaled, wk_ref[...])
    v = dot(scaled, wv_ref[...])
    first = lax.axis_index("core") == 0
    keep_out[...] = jnp.where(first, k, v).astype(BF)
    give_out[...] = jnp.where(first, v, k).astype(BF)


def message_kernel(scaled_ref, extra_ref, keep_ref, taken_ref, out_ref):
    terms = (keep_ref[...].astype(F32) + taken_ref[...].astype(F32)).astype(BF)
    for m, (z, _) in enumerate(PLACES):
        n = z // (ZS // HEADS)
        out_ref[m, 0:REQ, :] = scaled_ref[...]
        out_ref[m, REQ : 2 * REQ, :] = terms[:, n * HD : (n + 1) * HD]
        out_ref[m, 2 * REQ :, :] = extra_ref[...]


def tables_kernel(
    lengths_hbm, offload_hbm, host_hbm, slot_hbm, values_hbm,
    values_out, pick_ref, back_ref, cos_ref, sin_ref, span_ref,
    lengths_ref, offload_ref, host_ref, slot_ref, sems,
):
    pool, inst = lax.axis_index("pool"), lax.axis_index("inst")
    pairs = [(lengths_hbm, lengths_ref), (offload_hbm, offload_ref), (host_hbm, host_ref), (slot_hbm, slot_ref)]
    small = len(pairs)
    pairs.append((values_hbm.at[0, 0, :, :, head_lanes(lax.axis_index("z"))], values_out))
    copies = start_copies(pairs, sems)
    for copy in copies[:small]:
        copy.wait()
    yh = lax.axis_index("yh")
    home = (1 - yh) * (INSTS * REQ) + turn(iota((INSTS, REQ), 0)) * REQ + iota((INSTS, REQ), 1)
    away = yh * (INSTS * REQ) + turn(host_ref[...]) * REQ + slot_ref[...]
    seat = jnp.where(offload_ref[...] == 1, away, home)
    spans = lengths_ref[...].astype(F32)
    here = iota((REQ, REQ), 0) + ((1 ^ pool ^ yh) * INSTS + turn(inst)) * REQ
    square = iota((REQ, REQ), 0) == iota((REQ, REQ), 1)
    pick = jnp.zeros((REQ, POOLS * INSTS * REQ), F32)
    span = jnp.zeros((REQ, 1), F32)
    column = jnp.zeros((REQ, 1), F32)
    for i in range(INSTS):
        sits = seat[i : i + 1, :] == here
        wide = iota((REQ, POOLS * INSTS * REQ), 1) % (INSTS * REQ)
        place = (wide == iota(wide.shape, 0) + turn(i) * REQ).astype(F32).astype(BF)
        pick += dot(sits.astype(F32).astype(BF), place)
        span += jnp.sum(jnp.where(sits, spans[i : i + 1, :], 0.0), axis=1, keepdims=True)
        turned = jnp.sum(jnp.where(square, seat[i : i + 1, :].astype(F32), 0.0), axis=1, keepdims=True)
        column += jnp.where(inst == i, turned, 0.0)
    pick_ref[...] = pick.astype(BF)
    seats = iota((REQ, POOLS * INSTS * REQ), 1).astype(F32)
    back_ref[...] = (column == seats).astype(F32).astype(BF)
    half = HD // 2
    lanes = iota((REQ, HD), 1)
    frequency = jnp.exp((lanes % half).astype(F32) * (-2.0 / HD * 13.122363377404328))
    angles = span * frequency
    cos_ref[...] = jnp.cos(angles)
    sin_ref[...] = jnp.where(lanes < half, -jnp.sin(angles), jnp.sin(angles))
    span_ref[...] = jnp.broadcast_to(span, (REQ, HD))
    for copy in copies[small:]:
        copy.wait()


def query_kernel(own_ref, other_ref, wq_ref, out_ref):
    core = lax.axis_index("core")
    side = lax.axis_index("pool") ^ lax.axis_index("yh")
    q = jnp.zeros((REQ, HD), F32)
    own = jnp.zeros((REQ, HD), F32)
    other = jnp.zeros((REQ, HD), F32)
    extra = jnp.zeros((EXTRA, HD), F32)
    for m, (z, y) in enumerate(PLACES):
        weight = jnp.concatenate([wq_ref[y ^ side, z, y, c] for c in (core, 1 - core)], axis=0)
        features = jnp.concatenate([own_ref[m, 0:REQ, :], other_ref[m, 0:REQ, :]], axis=1)
        q += dot(features, weight)
        own += own_ref[m, REQ : 2 * REQ, :].astype(F32)
        other += other_ref[m, REQ : 2 * REQ, :].astype(F32)
        extra += own_ref[m, 2 * REQ :, :].astype(F32) + other_ref[m, 2 * REQ :, :].astype(F32)
    first = core == 0
    k, v = jnp.where(first, own, other), jnp.where(first, other, own)
    rest = two_rows(extra[0:1] + extra[1:2])
    for m in range(POOLS * INSTS):
        for n, part in enumerate((q, k, v)):
            out_ref[m, n * REQ : (n + 1) * REQ, :] = part.astype(BF)
        out_ref[m, 3 * REQ :, :] = rest


def attend_kernel(got_ref, keys_ref, values_ref, pick_ref, cos_ref, sin_ref, span_ref, out_ref, *, width):
    pick = pick_ref[...]
    q, k, v = (dot(pick, got_ref[:, n * REQ : (n + 1) * REQ, :].reshape(pick.shape[1], HD)) for n in range(3))
    rest = jnp.zeros((EXTRA, HD), F32)
    for m in range(POOLS * INSTS):
        rest += got_ref[m, 3 * REQ :, :].astype(F32)
    squares = jnp.sum(pick[:, :HD].astype(F32) * (rest[0:1] + rest[1:2]), axis=1, keepdims=True)
    root = jnp.sqrt(squares / width + epsilon)

    def rotate(t):
        return t * cos_ref[...] + pltpu.roll(t, HD // 2, 1) * sin_ref[...]

    q = rotate(q).astype(BF)
    k = rotate(k).astype(BF)
    v = (v / root).astype(BF)
    lanes = head_lanes(lax.axis_index("z"))
    keys = keys_ref[0, 0, :, :, lanes].reshape(REQ * HD, HD)
    values = values_ref[...].reshape(REQ * HD, HD)
    every = lax.dot_general(q, keys, (((1,), (1,)), ((), ())), preferred_element_type=F32)
    request = iota((8, HD), 0)
    rows = []
    for group in range(REQ // 8):
        block = jnp.zeros((8, HD), F32)
        for n in range(8):
            r = group * 8 + n
            block = jnp.where(request == n, every[group * 8 : group * 8 + 8, r * HD : (r + 1) * HD], block)
        rows.append(block)
    scale = HD ** (-0.5) / root
    scores = jnp.concatenate(rows, axis=0) * scale
    own_score = jnp.sum(q.astype(F32) * k.astype(F32), axis=1, keepdims=True) * (scale / root)
    visible = iota((REQ, HD), 1).astype(F32) < span_ref[...]
    scores = jnp.where(visible, scores, -jnp.inf)
    peak = jnp.maximum(jnp.max(scores, axis=1, keepdims=True), -1e30)
    exps = jnp.exp(scores - peak)
    request = iota((REQ, HD), 0)
    spread = jnp.concatenate([jnp.where(request == r, exps, 0.0).astype(BF) for r in range(REQ)], axis=1)
    mixed = dot(spread, values)
    top = jnp.maximum(peak, own_score)
    cached, own = jnp.exp(peak - top), jnp.exp(own_score - top)
    total = jnp.sum(exps, axis=1, keepdims=True) * cached + own
    mixed = (mixed * (cached / total) + (own / total) * v.astype(F32)).astype(BF)
    for m in range(POOLS * INSTS * CORES):
        out_ref[m] = mixed


def output_kernel(got_ref, back_ref, own_ref, other_ref, out_ref):
    core = lax.axis_index("core")
    back = back_ref[...]
    seats = POOLS * INSTS * REQ
    mine = dot(back, got_ref[:, core].reshape(seats, HD)).astype(BF)
    buddy = dot(back, got_ref[:, 1 - core].reshape(seats, HD)).astype(BF)
    side = lax.axis_index("pool") ^ lax.axis_index("yh")
    rows = jnp.concatenate([mine, buddy], axis=1)
    parts = []
    for m in range(0, RING, 2):
        weights = []
        for z, y in PLACES[m : m + 2]:
            block = (((y ^ side) * ZS + z) * YS + y) * CORES + core
            lanes = pl.ds(pl.multiple_of(block * HD, HD), HD)
            weights.append(jnp.concatenate([own_ref[:, lanes], other_ref[:, lanes]], axis=0))
        two = dot(rows, jnp.concatenate(weights, axis=1)).astype(BF)
        parts += [two[:, :HD], two[:, HD:]]
    for m, part in enumerate(parts):
        out_ref[m] = part


def sum_kernel(got_ref, out_ref):
    total = got_ref[0].astype(F32)
    for m in range(1, RING):
        total += got_ref[m].astype(F32)
    out_ref[0] = total.astype(BF)


def in_hbm(*arrays):
    return [pltpu.with_memory_space_constraint(a, pltpu.HBM) for a in arrays]


def call(kernel, shapes, specs, flops, moved, scratch=(), limit=24):
    one = not isinstance(shapes, list)
    return pl.pallas_call(
        kernel,
        out_shape=shapes if one else tuple(shapes),
        in_specs=specs,
        out_specs=VMEM if one else tuple(VMEM for _ in shapes),
        scratch_shapes=list(scratch),
        cost_estimate=pl.CostEstimate(flops=flops, bytes_accessed=moved, transcendentals=0),
        compiler_params=pltpu.CompilerParams(vmem_limit_bytes=limit << 20),
    )


def shape(*dims, dtype=BF):
    return jax.ShapeDtypeStruct(dims, dtype)


def shards(
    hidden_states,
    norm_gain,
    query_weight,
    key_weight,
    value_weight,
    output_weight,
    key_cache,
    value_cache,
    lengths,
    offload,
    host_instance,
    cache_slot,
):
    width = query_weight.shape[0]
    seats = POOLS * INSTS * REQ

    scaled, extra, keep, give = call(
        features_kernel,
        [shape(REQ, HD), shape(EXTRA, HD), shape(REQ, HEADS * HD), shape(REQ, HEADS * HD)],
        [HBM] * 4,
        1 << 23,
        1 << 20,
        [
            pltpu.VMEM((1, REQ, HD), BF),
            pltpu.VMEM((1, HD), BF),
            pltpu.VMEM(key_weight.shape, BF),
            pltpu.VMEM(value_weight.shape, BF),
            pltpu.SemaphoreType.DMA((4,)),
        ],
    )(*in_hbm(hidden_states, norm_gain.reshape(1, HD), key_weight, value_weight))
    message = call(message_kernel, shape(RING, 2 * REQ + EXTRA, HD), [VMEM] * 4, 1 << 14, 1 << 19)(
        scaled, extra, keep, swap_core(give)
    )
    message, output_weight = lax.optimization_barrier((message, output_weight))
    buddy_weight = swap_core(output_weight)
    got = exchange(message, RINGS)
    got, lengths, key_cache = lax.optimization_barrier((got, lengths, key_cache))
    other = swap_core(got)
    table = pltpu.VMEM(lengths.shape, I32)
    tables = call(
        tables_kernel,
        [
            shape(REQ, HD, HD),
            shape(REQ, seats),
            shape(REQ, seats),
            shape(REQ, HD, dtype=F32),
            shape(REQ, HD, dtype=F32),
            shape(REQ, HD, dtype=F32),
        ],
        [HBM] * 5,
        1 << 22,
        1 << 22,
        [table] * 4 + [pltpu.SemaphoreType.DMA((5,))],
    )(
        *in_hbm(
            lengths,
            offload,
            host_instance,
            cache_slot,
            value_cache,
        )
    )
    other, tables, buddy_weight = lax.optimization_barrier((other, tables, buddy_weight))
    values, pick, back, cos, sin, span = tables
    message = call(query_kernel, shape(POOLS * INSTS, 3 * REQ + EXTRA, HD), [VMEM] * 3, 1 << 25, 1 << 22)(got, other, query_weight.reshape(POOLS, ZS, YS, CORES, HD, HD))
    got = exchange(message, HOSTS)
    message = call(
        functools.partial(attend_kernel, width=width), shape(POOLS * INSTS * CORES, REQ, HD), [VMEM] * 7, 1 << 26, 1 << 22
    )(got, key_cache, values, pick, cos, sin, span)
    got = exchange(message, CHIPS)
    message = call(output_kernel, shape(RING, REQ, HD), [VMEM] * 4, 1 << 25, 1 << 22)(
        got.reshape(POOLS * INSTS, CORES, REQ, HD), back, output_weight, buddy_weight
    )
    got = exchange(message, RINGS)
    return call(sum_kernel, shape(1, REQ, HD), [VMEM], 1 << 17, 1 << 18)(got)


def solution(mesh):
    finer = Mesh(mesh.devices.reshape(SIZES), AXES)
    in_specs = (
        P("inst", None, ("pool",) + TP),
        P(("pool",) + TP),
        P(None, TP),
        P(("pool",) + TP, None),
        P(("pool",) + TP, None),
        P(TP, None),
        P("pool", "inst", None, None, None),
        P("pool", "inst", None, None, None),
        P(),
        P(),
        P(),
        P(),
    )
    out_specs = P("inst", None, ("pool",) + TP)
    return jax.shard_map(shards, mesh=finer, in_specs=in_specs, out_specs=out_specs, check_vma=False)
```
